32 devices in a mesh: samp: 16 (over z, x, core), snp: 2 (over y).
Axes of the slice: x: 2, y: 2, z: 4, core: 2. Of those that a mesh axis runs over, the one named last changes fastest.
Arguments:
- genotype: int32 [10240, 4096], P('samp', 'snp'), may hold values from 0 to 2
- freqs: float32 [4096], P('snp'), may hold values from 0.35 to 0.65
- left_factors: float32 [10240, 20], P('samp'), may hold values from -6 to 6
- singular: float32 [20], replicated, may hold values from 0.5 to 2
- right_factors: float32 [4096, 20], P(('snp', 'samp')), may hold values from -1.25 to 1.25
- sketch: bfloat16 [4096, 64], P('snp'), may hold values from -6 to 6
- batch_sizes: int32 [12], replicated, may hold values from 1 to 1706, 10240 in all
- missing_batch: int32 [48], replicated, may hold values from 0 to 11, as said below
- missing_block: int32 [48], replicated, may hold values from 0 to 15, as said below
Outputs:
- basis: float32 [10240, 64], P('samp')
- projection: float32 [4096, 64], P('snp')
- snp_basis: float32 [4096, 64], P('snp')
The draws below stay inside these ranges and needn't reach their ends.
Inputs may be any that keep to these rules, and one draw needn't show every extreme that they name: The pairs (missing_batch, missing_block) are distinct; every block id appears exactly 3 times and every batch id exactly 48 // 12 times. `missing_block`: paired entry by entry with missing_batch.
All inputs are finite; a program needn't handle non-finite values.
Results may differ from the reference program's by a relative error of at most 0.012.
Values may be sent and summed in bfloat16 or wider, within the bound.
A program may use at most 64 MiB of HBM per device.

```python
import math
import jax
import jax.numpy as jnp
import numpy as np
from jax import lax

SNPS = 4096
RANK = 20
SKETCH = 64
BATCHES = 12
BLOCK = 256
ITERS = 2
ROWS_DEV = 640
BLOCKS = 16
MISS = 48
NSAMP = 10240


def missing_tiles(key):
    offset = jax.random.randint(jax.random.fold_in(key, 11), (), 0, BATCHES)
    order = jax.random.permutation(jax.random.fold_in(key, 12), MISS).astype(jnp.int32)
    block_ids = order // 3
    turn = order % 3
    batch_ids = (offset + block_ids + BATCHES // 3 * turn) % BATCHES
    return (batch_ids.astype(jnp.int32), block_ids.astype(jnp.int32))


def draw_missing_batch(key, part):
    return missing_tiles(key)[0]


def draw_missing_block(key, part):
    return missing_tiles(key)[1]


def draw_genotype(key, part):
    populations = jax.random.randint(jax.random.fold_in(key, 21), (NSAMP,), 0, 4).astype(jnp.int32)
    base_rate = jax.random.randint(jax.random.fold_in(key, 22), (SNPS,), 350, 651).astype(jnp.int32)
    shifts = jax.random.randint(jax.random.fold_in(key, 23), (4, SNPS), -150, 151).astype(jnp.int32)
    permille = base_rate[None, :] + shifts[populations]
    pairs = jax.random.randint(jax.random.fold_in(key, 24), (NSAMP, SNPS), 0, 1000000).astype(jnp.int32)
    first = (pairs // 1000 < permille).astype(jnp.int32)
    second = (pairs % 1000 < permille).astype(jnp.int32)
    return (first + second).astype(jnp.int32)


def block_scale(rng, extent, split, least, top_value):
    factor_of, own = 1.0, jax.random.fold_in(rng, 6)
    for axis_at, blocks in split:
        draws = jnp.exp(jax.random.uniform(jax.random.fold_in(own, axis_at), (blocks,), jnp.float32, least / len(split), top_value / len(split)))
        factor_of = factor_of * jnp.repeat(draws, extent[axis_at] // blocks).reshape([-1 if axis == axis_at else 1 for axis in range(len(extent))])
    return factor_of


def length_profile(count, total, most, skew):
    loads = [(1 << 20) // math.isqrt(grade ** skew) + 1 for grade in range(2, count + 1)]
    spare, given = total - most - (count - 1), [1] * (count - 1)
    while spare > 0:
        movable = [i for i in range(count - 1) if given[i] < most]
        whole, budget = sum([loads[i] for i in movable]), spare
        for i in movable:
            more = min(most - given[i], max(1, budget * loads[i] // whole), spare)
            given[i] = given[i] + more
            spare = spare - more
    return np.array([most] + given)


def uneven(key, amount, total, reach, lean):
    if amount == 2:
        one = jax.random.randint(key, (), max(1, total - reach), min(reach, total - 1) + 1)
        return jnp.stack([one, total - one])
    sizes = jnp.asarray(length_profile(amount, total, reach, lean), jnp.int32)
    pairs = (amount - 1) // 2
    source_of, receiver = sizes[1:1 + 2 * pairs:2], sizes[2:2 + 2 * pairs:2]
    room = jnp.minimum(source_of - 1, reach - receiver)
    moved = jax.random.randint(jax.random.fold_in(key, 1), (pairs,), 0, 1 << 20) % (room + 1)
    sizes = sizes.at[1:1 + 2 * pairs:2].set(source_of - moved).at[2:2 + 2 * pairs:2].set(receiver + moved)
    return sizes[jax.random.permutation(jax.random.fold_in(key, 2), amount)]


def normal_values(stream_key, extent, width, bound, cuts=(), held_as=jnp.bfloat16):
    entries = jax.random.normal(stream_key, extent, jnp.float32) * width
    if len(cuts) > 0:
        entries = block_scale(stream_key, extent, cuts, -0.22, 0.18) * entries
    return jnp.clip(entries, min=-bound, max=bound).astype(held_as)


def setup_inputs(seed: int = 0) -> dict:
    splits = jax.random.split(jax.random.key(seed), 10)
    return {
        "genotype": draw_genotype(jax.random.fold_in(splits[9], 71), 0),
        "freqs": jnp.clip(0.35 + 0.29999998 * jax.random.uniform(splits[1], (SNPS,), jnp.float32) ** block_scale(splits[1], (SNPS,), ((0, 2),), -0.2, 0.2), 0.35, 0.65),
        "left_factors": normal_values(splits[2], (NSAMP, RANK), 1.0, 6.0, ((0, 16),), jnp.float32),
        "singular": jnp.clip(jnp.exp(jax.random.uniform(splits[3], (RANK,), jnp.float32, math.log(0.5), math.log(2.0))), 0.5, 2.0),
        "right_factors": normal_values(splits[4], (SNPS, RANK), RANK ** -0.5, 1.25, ((0, 32),), jnp.float32),
        "sketch": normal_values(splits[5], (SNPS, SKETCH), 1.0, 6.0, ((0, 2),)),
        "batch_sizes": uneven(splits[6], BATCHES, NSAMP, NSAMP // 6, 2).astype(jnp.int32),
        "missing_batch": draw_missing_batch(jax.random.fold_in(splits[9], 71), 0),
        "missing_block": draw_missing_block(jax.random.fold_in(splits[9], 71), 0),
    }


def orthonormal(values, total):
    gram = jnp.dot(values.T, values, precision=lax.Precision.HIGHEST) / total
    lower = jnp.linalg.cholesky(gram)
    return jax.scipy.linalg.solve_triangular(lower, values.T, lower=True).T

def orthonormal_reversed(values, total):
    return orthonormal(values[:, ::-1], total)[:, ::-1]

def reference(genotype, freqs, left_factors, singular, right_factors, sketch, batch_sizes, missing_batch, missing_block):
    batch_range = jnp.arange(BATCHES, dtype=jnp.int32)
    block_range = jnp.arange(BLOCKS, dtype=jnp.int32)
    hot_batch = (missing_batch[:, None] == batch_range[None, :]).astype(jnp.float32)
    hot_block = (missing_block[:, None] == block_range[None, :]).astype(jnp.float32)
    table = jnp.dot(hot_batch.T.astype(jnp.float32), hot_block.astype(jnp.float32), preferred_element_type=jnp.float32)
    ends = jnp.cumsum(batch_sizes).astype(jnp.int32)
    col_block = (jnp.arange(SNPS, dtype=jnp.int32) // BLOCK).astype(jnp.int32)
    col_hot = (col_block[None, :] == block_range[:, None]).astype(jnp.float32)
    weighted = left_factors * singular[None, :]

    def build(index):
        start = (index * ROWS_DEV).astype(jnp.int32)
        geno_rows = lax.dynamic_slice_in_dim(genotype, start, ROWS_DEV, 0)
        weight_rows = lax.dynamic_slice_in_dim(weighted, start, ROWS_DEV, 0)
        row_ids = start + jnp.arange(ROWS_DEV, dtype=jnp.int32)
        batch_of = lax.optimization_barrier(jnp.sum((row_ids[:, None] >= ends[None, :]).astype(jnp.int32), axis=1)).astype(jnp.int32)
        row_hot = (batch_of[:, None] == batch_range[None, :]).astype(jnp.float32)
        missing = jnp.dot(jnp.dot(row_hot.astype(jnp.float32), table.astype(jnp.float32), preferred_element_type=jnp.float32).astype(jnp.float32), col_hot.astype(jnp.float32), preferred_element_type=jnp.float32) > 0.5
        lowrank = jnp.dot(weight_rows, right_factors.T, precision=lax.Precision.HIGHEST)
        observed = geno_rows.astype(jnp.float32) - 2.0 * freqs[None, :]
        return jnp.where(missing, lowrank, observed).astype(jnp.bfloat16)
    pieces = lax.map(build, jnp.arange(NSAMP // ROWS_DEV, dtype=jnp.int32))
    matrix = pieces.reshape(NSAMP, SNPS)
    basis = orthonormal(jnp.dot(matrix.astype(jnp.float32), sketch.astype(jnp.float32), preferred_element_type=jnp.float32), NSAMP)
    column_basis = jnp.zeros((SNPS, SKETCH), jnp.float32)
    for sweep_index in range(ITERS):
        columns = jnp.dot(matrix.T.astype(jnp.float32), basis.astype(jnp.bfloat16).astype(jnp.float32), preferred_element_type=jnp.float32)
        column_basis = orthonormal_reversed(columns, SNPS)
        basis = orthonormal(jnp.dot(matrix.astype(jnp.float32), column_basis.astype(jnp.bfloat16).astype(jnp.float32), preferred_element_type=jnp.float32), NSAMP)
    projection = jnp.dot(matrix.T.astype(jnp.float32), basis.astype(jnp.bfloat16).astype(jnp.float32), preferred_element_type=jnp.float32) / math.sqrt(NSAMP)
    return (basis, projection, column_basis)
```

```python
import functools
import math

import jax
import jax.numpy as jnp
from jax import lax
from jax.experimental import pallas as pl
from jax.experimental.pallas import tpu as pltpu
from jax.sharding import PartitionSpec as P

BATCHES = 12
BLOCK = 256
ITERS = 2
MESH = pl.DeviceIdType.MESH
NT = (((1,), (1,)), ((), ()))
NN = (((1,), (0,)), ((), ()))
ROW_STEP = 128


def dot32(a, b):
    return lax.dot_general(
        a, b, NN, precision=lax.Precision.HIGHEST, preferred_element_type=jnp.float32
    )


def dot16(a, b, dims):
    return lax.dot_general(a, b, dims, preferred_element_type=jnp.float32)


def split2(v):
    hi = v.astype(jnp.bfloat16)
    lo = (v - hi.astype(jnp.float32)).astype(jnp.bfloat16)
    return hi, lo


def inverse_factor(gram, reverse):
    k = gram.shape[0]
    rows = lax.broadcasted_iota(jnp.int32, (k, 2 * k), 0)
    lanes = lax.broadcasted_iota(jnp.int32, (k, 2 * k), 1)
    row1 = lax.broadcasted_iota(jnp.int32, (k, 1), 0)
    unit = (lanes == rows + k).astype(jnp.float32)
    a = jnp.concatenate([gram, unit[:, k:]], axis=1)
    order = range(k - 1, 0, -1) if reverse else range(k - 1)
    for j in order:
        pivot = a[j : j + 1, j : j + 1]
        after = row1 < j if reverse else row1 > j
        factor = jnp.where(after, a[:, j : j + 1] * (1.0 / pivot), 0.0)
        a = a - factor * a[j : j + 1, :]
    diag = jnp.sum(jnp.where(lanes == rows, a, 0.0), axis=1, keepdims=True)
    return a[:, k:] * lax.rsqrt(diag)


def kernel(
    n,
    m,
    sample_count,
    snp_count,
    geno_ref,
    freqs_ref,
    lw_ref,
    right_ref,
    sketch_ref,
    mask_ref,
    basis_ref,
    proj_ref,
    snpb_ref,
    geno,
    x_ref,
    rg,
    rt,
    ysl,
    gsl,
    t_src,
    t_dst,
    gr_src,
    gr_dst,
    ga_src,
    ga_dst,
    gfull,
    zg,
    zt,
    geno_sem,
    rg_send,
    rg_recv,
    y_send,
    y_recv,
    gz_send,
    gz_recv,
    t_send,
    t_recv,
    gr_send,
    gr_recv,
    ga_send,
    ga_recv,
    z_send,
    z_recv,
):
    me = lax.axis_index("samp")
    my = lax.axis_index("snp")
    rows, cols = x_ref.shape
    k = sketch_ref.shape[1]
    width = cols // n
    steps = rows // ROW_STEP

    def geno_copy(i):
        at = pl.ds(i * ROW_STEP, ROW_STEP)
        return pltpu.make_async_copy(geno_ref.at[at], geno.at[at], geno_sem.at[i])

    for i in range(steps):
        geno_copy(i).start()

    barrier = pltpu.get_barrier_semaphore()

    def greet_samp(o, c):
        pl.semaphore_signal(
            barrier, inc=1, device_id={"samp": lax.rem(me + o, n)}, device_id_type=MESH
        )
        return c

    def greet_snp(o, c):
        pl.semaphore_signal(
            barrier, inc=1, device_id={"snp": lax.rem(my + o, m)}, device_id_type=MESH
        )
        return c

    lax.fori_loop(1, n, greet_samp, 0)
    lax.fori_loop(1, m, greet_snp, 0)
    pl.semaphore_wait(barrier, n + m - 2)

    def remote(src, dst, send, recv, axis, peer):
        return pltpu.make_async_remote_copy(
            src_ref=src,
            dst_ref=dst,
            send_sem=send,
            recv_sem=recv,
            device_id={axis: peer},
            device_id_type=MESH,
        )

    def start_all(axis, size, mine, src_of, dst, send, recv):
        def body(o, c):
            peer = lax.rem(mine + o, size)
            remote(src_of(peer), dst.at[mine], send.at[o], recv.at[o], axis, peer).start()
            return c

        lax.fori_loop(1, size, body, 0)

    def wait_all(axis, size, mine, src_of, dst, send, recv):
        def body(o, c):
            peer = lax.rem(mine + o, size)
            source = lax.rem(mine + size - o, size)
            remote(src_of(peer), dst.at[source], send.at[o], recv.at[o], axis, peer).wait()
            return c

        lax.fori_loop(1, size, body, 0)

    def one(ref):
        return lambda peer: ref

    def per_peer(ref):
        return lambda peer: ref.at[peer]

    rg_args = ("samp", n, me, one(right_ref), rg, rg_send, rg_recv)
    start_all(*rg_args)
    rg[me] = right_ref[...]
    sketch_t = sketch_ref[...].astype(jnp.float32).T.astype(jnp.bfloat16)
    wait_all(*rg_args)
    depth = right_ref.shape[0]
    for p in range(n):
        piece = rg[p]
        b1 = piece.astype(jnp.bfloat16)
        r1 = piece - b1.astype(jnp.float32)
        b2 = r1.astype(jnp.bfloat16)
        b3 = (r1 - b2.astype(jnp.float32)).astype(jnp.bfloat16)
        for i, part in enumerate((b1, b2, b1, b3, b2, b1)):
            rt[i * depth : (i + 1) * depth, p * width : (p + 1) * width] = part

    def build(i, c):
        geno_copy(i).wait()
        at = pl.ds(pl.multiple_of(i * ROW_STEP, ROW_STEP), ROW_STEP)
        for b in range(cols // BLOCK):
            cut = slice(b * BLOCK, (b + 1) * BLOCK)
            lowrank = dot16(lw_ref[at, :], rt[:, cut], NN)
            observed = geno[at, cut].astype(jnp.float32) - 2.0 * freqs_ref[:, cut]
            gone = mask_ref[at, b : b + 1] > 0.5
            x_ref[at, cut] = jnp.where(gone, lowrank, observed).astype(jnp.bfloat16)
        return c

    lax.fori_loop(0, steps, build, 0)

    def snp_sum(value, slots, send, recv):
        slots[my] = value
        args = ("snp", m, my, one(slots.at[my]), slots, send, recv)
        start_all(*args)

        def finish():
            wait_all(*args)
            total = slots[0]
            for q in range(1, m):
                total = total + slots[q]
            return total

        return finish

    y = snp_sum(dot16(sketch_t, x_ref[...], NT), ysl.at[0], y_send.at[0], y_recv.at[0])()
    piece_rows = k // n
    for it in range(ITERS + 1):
        hi, lo = split2(y)
        both = jnp.concatenate([hi, lo], axis=0)
        g4 = dot16(both, both, NT)
        gram = g4[:k, :k] + (g4[:k, k:] + g4[k:, :k])
        for p in range(n):
            gr_src[it, p] = gram[p * piece_rows : (p + 1) * piece_rows]
        gr_args = ("samp", n, me, per_peer(gr_src.at[it]), gr_dst.at[it], gr_send.at[it], gr_recv.at[it])
        start_all(*gr_args)

        t2 = dot16(both, x_ref[...], NN)
        t = t2[:k] + t2[k:]
        for p in range(n):
            t_src[it, p] = t[:, p * width : (p + 1) * width]
        t_args = ("samp", n, me, per_peer(t_src.at[it]), t_dst.at[it], t_send.at[it], t_recv.at[it])
        start_all(*t_args)

        wait_all(*gr_args)
        gr_dst[it, me] = gr_src[it, me]
        piece = gr_dst[it, 0]
        for p in range(1, n):
            piece = piece + gr_dst[it, p]
        ga_src[it] = piece
        ga_args = ("samp", n, me, one(ga_src.at[it]), ga_dst.at[it], ga_send.at[it], ga_recv.at[it])
        start_all(*ga_args)
        ga_dst[it, me] = piece
        if it == ITERS:
            snpb_ref[...] = dot32(upper, zt[...].astype(jnp.float32))
        wait_all(*ga_args)
        for p in range(n):
            gfull[p * piece_rows : (p + 1) * piece_rows, :] = ga_dst[it, p]
        lower = inverse_factor(gfull[...] * (1.0 / sample_count), False)

        wait_all(*t_args)
        t_dst[it, me] = t_src[it, me]
        chunk = t_dst[it, 0]
        for p in range(1, n):
            chunk = chunk + t_dst[it, p]
        z = dot32(lower, chunk)
        if it == ITERS:
            z = z * (1.0 / math.sqrt(sample_count))
        zg[it, me] = z.astype(jnp.bfloat16)
        z_args = ("samp", n, me, one(zg.at[it, me]), zg.at[it], z_send.at[it], z_recv.at[it])
        start_all(*z_args)
        if it == ITERS:
            basis_ref[...] = dot32(lower, y)
            wait_all(*z_args)
            for p in range(n):
                proj_ref[:, p * width : (p + 1) * width] = zg[it, p].astype(jnp.float32)
            return
        wait_all(*z_args)
        for p in range(n):
            zt[:, p * width : (p + 1) * width] = zg[it, p]
        zz = zt[...]
        gz_done = snp_sum(dot16(zz, zz, NT), gsl.at[it], gz_send.at[it], gz_recv.at[it])
        v_done = snp_sum(
            dot16(zz, x_ref[...], NT), ysl.at[it + 1], y_send.at[it + 1], y_recv.at[it + 1]
        )
        upper = inverse_factor(gz_done() * (1.0 / snp_count), True)
        y = dot32(upper, v_done())


def on_device(
    n,
    m,
    genotype,
    freqs,
    left_factors,
    singular,
    right_factors,
    sketch,
    batch_sizes,
    missing_batch,
    missing_block,
):
    rows, cols = genotype.shape
    k = sketch.shape[1]
    rank = left_factors.shape[1]
    depth = -(-rank // 32) * 32
    width = cols // n
    batch_range = jnp.arange(BATCHES, dtype=jnp.int32)
    upto = batch_range[:, None] >= batch_range[None, :]
    ends = jnp.sum(jnp.where(upto, batch_sizes[None, :], 0), axis=1)
    begins = ends - batch_sizes
    hot = missing_batch[:, None] == batch_range[None, :]
    first = jnp.sum(jnp.where(hot, begins[None, :], 0), axis=1)
    last = jnp.sum(jnp.where(hot, ends[None, :], 0), axis=1)
    row_ids = lax.axis_index("samp") * rows + jnp.arange(rows, dtype=jnp.int32)
    inside = (row_ids[:, None] >= first[None, :]) & (row_ids[:, None] < last[None, :])
    local_block = missing_block - lax.axis_index("snp") * (cols // BLOCK)
    hot_block = local_block[:, None] == jnp.arange(128, dtype=jnp.int32)[None, :]
    mask = jnp.dot(
        inside.astype(jnp.bfloat16),
        hot_block.astype(jnp.bfloat16),
        preferred_element_type=jnp.float32,
    )

    weighted = jnp.pad(left_factors * singular[None, :], ((0, 0), (0, depth - rank)))
    a1 = lax.reduce_precision(weighted, 8, 7)
    a2 = lax.reduce_precision(weighted - a1, 8, 7)
    a3 = lax.reduce_precision(weighted - a1 - a2, 8, 7)
    lw = jnp.concatenate([a1, a1, a2, a1, a2, a3], axis=1).astype(jnp.bfloat16)
    right_t = jnp.pad(right_factors.T, ((0, depth - rank), (0, 0)))

    f32, b16 = jnp.float32, jnp.bfloat16
    vm = pl.BlockSpec(memory_space=pltpu.VMEM)
    dma = pltpu.SemaphoreType.DMA
    loops = ITERS + 1
    piece = k // n
    basis_t, proj_t, snpb_t = pl.pallas_call(
        functools.partial(
            kernel,
            n,
            m,
            float(rows * n),
            float(cols * m),
        ),
        out_shape=(
            jax.ShapeDtypeStruct((k, rows), f32),
            jax.ShapeDtypeStruct((k, cols), f32),
            jax.ShapeDtypeStruct((k, cols), f32),
        ),
        in_specs=[pl.BlockSpec(memory_space=pl.ANY)] + [vm] * 5,
        out_specs=(vm, vm, vm),
        scratch_shapes=[
            pltpu.VMEM((rows, cols), jnp.int32),
            pltpu.VMEM((rows, cols), b16),
            pltpu.VMEM((n, depth, width), f32),
            pltpu.VMEM((6 * depth, cols), b16),
            pltpu.VMEM((loops, m, k, rows), f32),
            pltpu.VMEM((ITERS, m, k, k), f32),
            pltpu.VMEM((loops, n, k, width), f32),
            pltpu.VMEM((loops, n, k, width), f32),
            pltpu.VMEM((loops, n, piece, k), f32),
            pltpu.VMEM((loops, n, piece, k), f32),
            pltpu.VMEM((loops, piece, k), f32),
            pltpu.VMEM((loops, n, piece, k), f32),
            pltpu.VMEM((k, k), f32),
            pltpu.VMEM((loops, n, k, width), b16),
            pltpu.VMEM((k, cols), b16),
            dma((rows // ROW_STEP,)),
            dma((n,)),
            dma((n,)),
            dma((loops, m)),
            dma((loops, m)),
            dma((ITERS, m)),
            dma((ITERS, m)),
            dma((loops, n)),
            dma((loops, n)),
            dma((loops, n)),
            dma((loops, n)),
            dma((loops, n)),
            dma((loops, n)),
            dma((loops, n)),
            dma((loops, n)),
        ],
        compiler_params=pltpu.CompilerParams(
            collective_id=0, has_side_effects=True, vmem_limit_bytes=48 * 1024 * 1024
        ),
        cost_estimate=pl.CostEstimate(
            flops=12 * rows * cols * k, bytes_accessed=4 * rows * cols, transcendentals=0
        ),
    )(genotype, freqs[None, :], lw, right_t, sketch, mask)
    return basis_t.T, proj_t.T, snpb_t.T


def solution(mesh):
    in_specs = (
        P("samp", "snp"),
        P("snp"),
        P("samp", None),
        P(),
        P(("snp", "samp"), None),
        P("snp", None),
        P(),
        P(),
        P(),
    )
    out_specs = (P("samp", None), P("snp", None), P("snp", None))
    body = functools.partial(on_device, mesh.shape["samp"], mesh.shape["snp"])
    return jax.shard_map(
        body, mesh=mesh, in_specs=in_specs, out_specs=out_specs, check_vma=False
    )
```

```python
import functools
import math

import jax
import jax.numpy as jnp
from jax import lax
from jax.experimental import pallas as pl
from jax.experimental.pallas import tpu as pltpu
from jax.sharding import PartitionSpec as P

BATCHES = 12
BLOCK = 256
ITERS = 2
MESH = pl.DeviceIdType.MESH
NT = (((1,), (1,)), ((), ()))
NN = (((1,), (0,)), ((), ()))
ROW_STEP = 128
GROUP = 8


def dot32(a, b):
    return lax.dot_general(
        a, b, NN, precision=lax.Precision.HIGHEST, preferred_element_type=jnp.float32
    )


def dot16(a, b, dims):
    return lax.dot_general(a, b, dims, preferred_element_type=jnp.float32)


def split2(v):
    hi = v.astype(jnp.bfloat16)
    lo = (v - hi.astype(jnp.float32)).astype(jnp.bfloat16)
    return hi, lo


def inverse_factor(gram, reverse):
    k = gram.shape[0]
    rows = lax.broadcasted_iota(jnp.int32, (k, 2 * k), 0)
    lanes = lax.broadcasted_iota(jnp.int32, (k, 2 * k), 1)
    unit = (lanes == rows + k).astype(jnp.float32)
    a = jnp.concatenate([gram, unit[:, k:]], axis=1)
    done = []
    for step in range(0, k, GROUP):
        count = a.shape[0]
        base = 0 if reverse else step
        local = lax.broadcasted_iota(jnp.int32, (count, 2 * k), 0)
        if reverse:
            group = [count - 1 - i for i in range(GROUP)]
        else:
            group = list(range(GROUP))
        columns = [
            jnp.broadcast_to(a[:, base + j : base + j + 1], (count, 2 * k)) for j in group
        ]
        for i, j in enumerate(group):
            after = local < j if reverse else local > j
            scale = 1.0 / columns[i][j : j + 1, :]
            factor = jnp.where(after, columns[i] * scale, 0.0)
            for later in range(i + 1, GROUP):
                columns[later] = columns[later] - factor * columns[later][j : j + 1, :]
            a = a - factor * a[j : j + 1, :]
        if reverse:
            done.insert(0, a[count - GROUP :])
            a = a[: count - GROUP]
        else:
            done.append(a[:GROUP])
            a = a[GROUP:]
    a = jnp.concatenate(done, axis=0)
    diag = jnp.sum(jnp.where(lanes == rows, a, 0.0), axis=1, keepdims=True)
    return a[:, k:] * lax.rsqrt(diag)


def kernel(
    n,
    m,
    sample_count,
    snp_count,
    geno_ref,
    freqs_ref,
    lw_ref,
    right_ref,
    sketch_ref,
    mask_ref,
    basis_ref,
    proj_ref,
    snpb_ref,
    geno,
    x_ref,
    rg,
    rt,
    ysl,
    gsl,
    t_src,
    t_half,
    t_sum,
    t_dst,
    gr_src,
    gr_dst,
    ga_src,
    ga_dst,
    gfull,
    zg,
    zt,
    geno_sem,
    rg_send,
    rg_recv,
    y_send,
    y_recv,
    gz_send,
    gz_recv,
    h_send,
    h_recv,
    t_send,
    t_recv,
    zh_send,
    zh_recv,
    gr_send,
    gr_recv,
    ga_send,
    ga_recv,
    z_send,
    z_recv,
):
    me = lax.axis_index("samp")
    my = lax.axis_index("snp")
    rows, cols = x_ref.shape
    k = sketch_ref.shape[1]
    width = cols // n
    steps = rows // ROW_STEP
    chips = n // 2
    half = cols // 2
    core = lax.rem(me, 2)
    chip = me // 2
    sibling = me + 1 - 2 * core

    def half_of(which):
        return pl.ds(pl.multiple_of(which * half, half), half)

    def geno_copy(i):
        at = pl.ds(i * ROW_STEP, ROW_STEP)
        return pltpu.make_async_copy(geno_ref.at[at], geno.at[at], geno_sem.at[i])

    for i in range(steps):
        geno_copy(i).start()

    barrier = pltpu.get_barrier_semaphore()

    def greet_samp(o, c):
        pl.semaphore_signal(
            barrier, inc=1, device_id={"samp": lax.rem(me + o, n)}, device_id_type=MESH
        )
        return c

    def greet_snp(o, c):
        pl.semaphore_signal(
            barrier, inc=1, device_id={"snp": lax.rem(my + o, m)}, device_id_type=MESH
        )
        return c

    lax.fori_loop(1, n, greet_samp, 0)
    lax.fori_loop(1, m, greet_snp, 0)
    pl.semaphore_wait(barrier, n + m - 2)

    def remote(src, dst, send, recv, axis, peer):
        return pltpu.make_async_remote_copy(
            src_ref=src,
            dst_ref=dst,
            send_sem=send,
            recv_sem=recv,
            device_id={axis: peer},
            device_id_type=MESH,
        )

    def start_all(axis, size, mine, src_of, dst, send, recv):
        def body(o, c):
            peer = lax.rem(mine + o, size)
            remote(src_of(peer), dst.at[mine], send.at[o], recv.at[o], axis, peer).start()
            return c

        lax.fori_loop(1, size, body, 0)

    def wait_all(axis, size, mine, src_of, dst, send, recv):
        def body(o, c):
            peer = lax.rem(mine + o, size)
            source = lax.rem(mine + size - o, size)
            remote(src_of(peer), dst.at[source], send.at[o], recv.at[o], axis, peer).wait()
            return c

        lax.fori_loop(1, size, body, 0)

    def start_chips(src_of, dst, send, recv):
        def body(o, c):
            to = lax.rem(chip + o, chips)
            remote(src_of(to), dst.at[chip], send.at[o], recv.at[o], "samp", 2 * to + core).start()
            return c

        lax.fori_loop(1, chips, body, 0)

    def wait_chips(src_of, dst, send, recv):
        def body(o, c):
            to = lax.rem(chip + o, chips)
            source = lax.rem(chip + chips - o, chips)
            remote(src_of(to), dst.at[source], send.at[o], recv.at[o], "samp", 2 * to + core).wait()
            return c

        lax.fori_loop(1, chips, body, 0)

    def one(ref):
        return lambda peer: ref

    def per_peer(ref):
        return lambda peer: ref.at[peer]

    rg_args = ("samp", n, me, one(right_ref), rg, rg_send, rg_recv)
    start_all(*rg_args)
    rg[me] = right_ref[...]
    sketch_t = sketch_ref[...].astype(jnp.float32).T.astype(jnp.bfloat16)
    wait_all(*rg_args)
    depth = right_ref.shape[0]
    for p in range(n):
        piece = rg[p]
        b1 = piece.astype(jnp.bfloat16)
        r1 = piece - b1.astype(jnp.float32)
        b2 = r1.astype(jnp.bfloat16)
        b3 = (r1 - b2.astype(jnp.float32)).astype(jnp.bfloat16)
        for i, part in enumerate((b1, b2, b1, b3, b2, b1)):
            rt[i * depth : (i + 1) * depth, p * width : (p + 1) * width] = part

    def build(i, c):
        geno_copy(i).wait()
        at = pl.ds(pl.multiple_of(i * ROW_STEP, ROW_STEP), ROW_STEP)
        for b in range(cols // BLOCK):
            cut = slice(b * BLOCK, (b + 1) * BLOCK)
            lowrank = dot16(lw_ref[at, :], rt[:, cut], NN)
            observed = geno[at, cut].astype(jnp.float32) - 2.0 * freqs_ref[:, cut]
            gone = mask_ref[at, b : b + 1] > 0.5
            x_ref[at, cut] = jnp.where(gone, lowrank, observed).astype(jnp.bfloat16)
        return c

    lax.fori_loop(0, steps, build, 0)

    def snp_sum(value, slots, send, recv):
        slots[my] = value
        args = ("snp", m, my, one(slots.at[my]), slots, send, recv)
        start_all(*args)

        def finish():
            wait_all(*args)
            total = slots[0]
            for q in range(1, m):
                total = total + slots[q]
            return total

        return finish

    y = snp_sum(dot16(sketch_t, x_ref[...], NT), ysl.at[0], y_send.at[0], y_recv.at[0])()
    piece_rows = k // n
    for it in range(ITERS + 1):
        hi, lo = split2(y)
        both = jnp.concatenate([hi, lo], axis=0)
        g4 = dot16(both, both, NT)
        gram = g4[:k, :k] + (g4[:k, k:] + g4[k:, :k])
        for p in range(n):
            gr_src[it, p] = gram[p * piece_rows : (p + 1) * piece_rows]
        gr_args = ("samp", n, me, per_peer(gr_src.at[it]), gr_dst.at[it], gr_send.at[it], gr_recv.at[it])
        start_all(*gr_args)

        def sketch_half(which):
            t2 = dot16(both, x_ref[:, half_of(which)], NN)
            return t2[:k] + t2[k:]

        t = sketch_half(1 - core)
        for p in range(chips):
            t_src[it, p] = t[:, p * width : (p + 1) * width]
        across = remote(
            t_src.at[it], t_half.at[it], h_send.at[it], h_recv.at[it], "samp", sibling
        )
        across.start()
        t = sketch_half(core)
        across.wait()
        for p in range(chips):
            t_sum[it, p] = t[:, p * width : (p + 1) * width] + t_half[it, p]
        t_args = (per_peer(t_sum.at[it]), t_dst.at[it], t_send.at[it], t_recv.at[it])
        start_chips(*t_args)

        wait_all(*gr_args)
        gr_dst[it, me] = gr_src[it, me]
        piece = gr_dst[it, 0]
        for p in range(1, n):
            piece = piece + gr_dst[it, p]
        ga_src[it] = piece
        ga_args = ("samp", n, me, one(ga_src.at[it]), ga_dst.at[it], ga_send.at[it], ga_recv.at[it])
        start_all(*ga_args)
        ga_dst[it, me] = piece
        if it == ITERS:
            for c in range(2):
                snpb_ref[:, c * half : (c + 1) * half] = dot32(upper, zt[c].astype(jnp.float32))
        wait_all(*ga_args)
        for p in range(n):
            gfull[p * piece_rows : (p + 1) * piece_rows, :] = ga_dst[it, p]
        lower = inverse_factor(gfull[...] * (1.0 / sample_count), False)

        wait_chips(*t_args)
        t_dst[it, chip] = t_sum[it, chip]
        chunk = t_dst[it, 0]
        for p in range(1, chips):
            chunk = chunk + t_dst[it, p]
        z = dot32(lower, chunk)
        if it == ITERS:
            z = z * (1.0 / math.sqrt(sample_count))
        zg[it, core, chip] = z.astype(jnp.bfloat16)
        z_args = (one(zg.at[it, core, chip]), zg.at[it, core], z_send.at[it], z_recv.at[it])
        start_chips(*z_args)
        if it == ITERS:
            basis_ref[...] = dot32(lower, y)
        wait_chips(*z_args)
        across = remote(
            zg.at[it, core], zg.at[it, core], zh_send.at[it], zh_recv.at[it], "samp", sibling
        )
        across.start()
        landed = remote(
            zg.at[it, core], zg.at[it, 1 - core], zh_send.at[it], zh_recv.at[it], "samp", sibling
        )
        if it == ITERS:
            landed.wait()
            for c in range(2):
                for p in range(chips):
                    at = c * half + p * width
                    proj_ref[:, at : at + width] = zg[it, c, p].astype(jnp.float32)
            return

        def use_half(which):
            for p in range(chips):
                zt[which, :, p * width : (p + 1) * width] = zg[it, which, p]
            zz = zt[which]
            return dot16(zz, zz, NT), dot16(zz, x_ref[:, half_of(which)], NT)

        gz_own, v_own = use_half(core)
        landed.wait()
        gz_far, v_far = use_half(1 - core)
        gz_done = snp_sum(gz_own + gz_far, gsl.at[it], gz_send.at[it], gz_recv.at[it])
        v_done = snp_sum(v_own + v_far, ysl.at[it + 1], y_send.at[it + 1], y_recv.at[it + 1])
        upper = inverse_factor(gz_done() * (1.0 / snp_count), True)
        y = dot32(upper, v_done())


def on_device(
    n,
    m,
    genotype,
    freqs,
    left_factors,
    singular,
    right_factors,
    sketch,
    batch_sizes,
    missing_batch,
    missing_block,
):
    rows, cols = genotype.shape
    k = sketch.shape[1]
    rank = left_factors.shape[1]
    depth = -(-rank // 32) * 32
    width = cols // n
    batch_range = jnp.arange(BATCHES, dtype=jnp.int32)
    upto = batch_range[:, None] >= batch_range[None, :]
    ends = jnp.sum(jnp.where(upto, batch_sizes[None, :], 0), axis=1)
    begins = ends - batch_sizes
    hot = missing_batch[:, None] == batch_range[None, :]
    first = jnp.sum(jnp.where(hot, begins[None, :], 0), axis=1)
    last = jnp.sum(jnp.where(hot, ends[None, :], 0), axis=1)
    row_ids = lax.axis_index("samp") * rows + jnp.arange(rows, dtype=jnp.int32)
    inside = (row_ids[:, None] >= first[None, :]) & (row_ids[:, None] < last[None, :])
    local_block = missing_block - lax.axis_index("snp") * (cols // BLOCK)
    hot_block = local_block[:, None] == jnp.arange(128, dtype=jnp.int32)[None, :]
    mask = jnp.dot(
        inside.astype(jnp.bfloat16),
        hot_block.astype(jnp.bfloat16),
        preferred_element_type=jnp.float32,
    )

    weighted = jnp.pad(left_factors * singular[None, :], ((0, 0), (0, depth - rank)))
    a1 = lax.reduce_precision(weighted, 8, 7)
    a2 = lax.reduce_precision(weighted - a1, 8, 7)
    a3 = lax.reduce_precision(weighted - a1 - a2, 8, 7)
    lw = jnp.concatenate([a1, a1, a2, a1, a2, a3], axis=1).astype(jnp.bfloat16)
    right_t = jnp.pad(right_factors.T, ((0, depth - rank), (0, 0)))

    f32, b16 = jnp.float32, jnp.bfloat16
    vm = pl.BlockSpec(memory_space=pltpu.VMEM)
    dma = pltpu.SemaphoreType.DMA
    loops = ITERS + 1
    piece = k // n
    basis_t, proj_t, snpb_t = pl.pallas_call(
        functools.partial(
            kernel,
            n,
            m,
            float(rows * n),
            float(cols * m),
        ),
        out_shape=(
            jax.ShapeDtypeStruct((k, rows), f32),
            jax.ShapeDtypeStruct((k, cols), f32),
            jax.ShapeDtypeStruct((k, cols), f32),
        ),
        in_specs=[pl.BlockSpec(memory_space=pl.ANY)] + [vm] * 5,
        out_specs=(vm, vm, vm),
        scratch_shapes=[
            pltpu.VMEM((rows, cols), jnp.int32),
            pltpu.VMEM((rows, cols), b16),
            pltpu.VMEM((n, depth, width), f32),
            pltpu.VMEM((6 * depth, cols), b16),
            pltpu.VMEM((loops, m, k, rows), f32),
            pltpu.VMEM((ITERS, m, k, k), f32),
            pltpu.VMEM((loops, n // 2, k, width), f32),
            pltpu.VMEM((loops, n // 2, k, width), f32),
            pltpu.VMEM((loops, n // 2, k, width), f32),
            pltpu.VMEM((loops, n // 2, k, width), f32),
            pltpu.VMEM((loops, n, piece, k), f32),
            pltpu.VMEM((loops, n, piece, k), f32),
            pltpu.VMEM((loops, piece, k), f32),
            pltpu.VMEM((loops, n, piece, k), f32),
            pltpu.VMEM((k, k), f32),
            pltpu.VMEM((loops, 2, n // 2, k, width), b16),
            pltpu.VMEM((2, k, cols // 2), b16),
            dma((rows // ROW_STEP,)),
            dma((n,)),
            dma((n,)),
            dma((loops, m)),
            dma((loops, m)),
            dma((ITERS, m)),
            dma((ITERS, m)),
            dma((loops,)),
            dma((loops,)),
            dma((loops, n // 2)),
            dma((loops, n // 2)),
            dma((loops,)),
            dma((loops,)),
            dma((loops, n)),
            dma((loops, n)),
            dma((loops, n)),
            dma((loops, n)),
            dma((loops, n // 2)),
            dma((loops, n // 2)),
        ],
        compiler_params=pltpu.CompilerParams(
            collective_id=0, has_side_effects=True, vmem_limit_bytes=48 * 1024 * 1024
        ),
        cost_estimate=pl.CostEstimate(
            flops=12 * rows * cols * k, bytes_accessed=4 * rows * cols, transcendentals=0
        ),
    )(genotype, freqs[None, :], lw, right_t, sketch, mask)
    return basis_t.T, proj_t.T, snpb_t.T


def solution(mesh):
    in_specs = (
        P("samp", "snp"),
        P("snp"),
        P("samp", None),
        P(),
        P(("snp", "samp"), None),
        P("snp", None),
        P(),
        P(),
        P(),
    )
    out_specs = (P("samp", None), P("snp", None), P("snp", None))
    body = functools.partial(on_device, mesh.shape["samp"], mesh.shape["snp"])
    return jax.shard_map(
        body, mesh=mesh, in_specs=in_specs, out_specs=out_specs, check_vma=False
    )
```

```python
import functools
import math

import jax
import jax.numpy as jnp
from jax import lax
from jax.experimental import pallas as pl
from jax.experimental.pallas import tpu as pltpu
from jax.sharding import PartitionSpec as P

BATCHES = 12
BLOCK = 256
ITERS = 2
MESH = pl.DeviceIdType.MESH
NT = (((1,), (1,)), ((), ()))
NN = (((1,), (0,)), ((), ()))
ROW_STEP = 128
GROUP = 8


def dot32(a, b):
    return lax.dot_general(
        a, b, NN, precision=lax.Precision.HIGHEST, preferred_element_type=jnp.float32
    )


def dot16(a, b, dims):
    return lax.dot_general(a, b, dims, preferred_element_type=jnp.float32)


def split2(v):
    hi = v.astype(jnp.bfloat16)
    lo = (v - hi.astype(jnp.float32)).astype(jnp.bfloat16)
    return hi, lo


def inverse_factor(gram, reverse):
    k = gram.shape[0]
    rows = lax.broadcasted_iota(jnp.int32, (k, 2 * k), 0)
    lanes = lax.broadcasted_iota(jnp.int32, (k, 2 * k), 1)
    unit = (lanes == rows + k).astype(jnp.float32)
    a = jnp.concatenate([gram, unit[:, k:]], axis=1)
    done = []
    for step in range(0, k, GROUP):
        count = a.shape[0]
        base = 0 if reverse else step
        local = lax.broadcasted_iota(jnp.int32, (count, 2 * k), 0)
        if reverse:
            group = [count - 1 - i for i in range(GROUP)]
        else:
            group = list(range(GROUP))
        columns = [
            jnp.broadcast_to(a[:, base + j : base + j + 1], (count, 2 * k)) for j in group
        ]
        for i, j in enumerate(group):
            after = local < j if reverse else local > j
            scale = 1.0 / columns[i][j : j + 1, :]
            factor = jnp.where(after, columns[i] * scale, 0.0)
            for later in range(i + 1, GROUP):
                columns[later] = columns[later] - factor * columns[later][j : j + 1, :]
            a = a - factor * a[j : j + 1, :]
        if reverse:
            done.insert(0, a[count - GROUP :])
            a = a[: count - GROUP]
        else:
            done.append(a[:GROUP])
            a = a[GROUP:]
    a = jnp.concatenate(done, axis=0)
    diag = jnp.sum(jnp.where(lanes == rows, a, 0.0), axis=1, keepdims=True)
    return a[:, k:] * lax.rsqrt(diag)


def kernel(
    n,
    m,
    sample_count,
    snp_count,
    geno_ref,
    freqs_ref,
    lw_ref,
    right_ref,
    sketch_ref,
    mask_ref,
    basis_ref,
    proj_ref,
    snpb_ref,
    geno,
    x_ref,
    rg,
    rt,
    yfirst,
    ysl,
    gsl,
    t_src,
    t_half,
    t_sum,
    t_dst,
    t_sum16,
    t_dst16,
    gr_src,
    gr_dst,
    ga_src,
    ga_dst,
    gfull,
    zg,
    zt,
    geno_sem,
    rg_send,
    rg_recv,
    rh_send,
    rh_recv,
    y_send,
    y_recv,
    gz_send,
    gz_recv,
    h_send,
    h_recv,
    t_send,
    t_recv,
    zh_send,
    zh_recv,
    gr_send,
    gr_recv,
    ga_send,
    ga_recv,
    z_send,
    z_recv,
):
    me = lax.axis_index("samp")
    my = lax.axis_index("snp")
    rows, cols = x_ref.shape
    k = sketch_ref.shape[1]
    width = cols // n
    steps = rows // ROW_STEP
    chips = n // 2
    half = cols // 2
    core = lax.rem(me, 2)
    chip = me // 2
    sibling = me + 1 - 2 * core

    def half_of(which):
        return pl.ds(pl.multiple_of(which * half, half), half)

    def geno_copy(i):
        at = pl.ds(i * ROW_STEP, ROW_STEP)
        return pltpu.make_async_copy(geno_ref.at[at], geno.at[at], geno_sem.at[i])

    for i in range(steps):
        geno_copy(i).start()

    barrier = pltpu.get_barrier_semaphore()

    def greet_samp(o, c):
        pl.semaphore_signal(
            barrier, inc=1, device_id={"samp": lax.rem(me + o, n)}, device_id_type=MESH
        )
        return c

    def greet_snp(o, c):
        pl.semaphore_signal(
            barrier, inc=1, device_id={"snp": lax.rem(my + o, m)}, device_id_type=MESH
        )
        return c

    lax.fori_loop(1, n, greet_samp, 0)
    lax.fori_loop(1, m, greet_snp, 0)
    pl.semaphore_wait(barrier, n + m - 2)

    def remote(src, dst, send, recv, axis, peer):
        return pltpu.make_async_remote_copy(
            src_ref=src,
            dst_ref=dst,
            send_sem=send,
            recv_sem=recv,
            device_id={axis: peer},
            device_id_type=MESH,
        )

    def start_all(axis, size, mine, src_of, dst, send, recv):
        def body(o, c):
            peer = lax.rem(mine + o, size)
            remote(src_of(peer), dst.at[mine], send.at[o], recv.at[o], axis, peer).start()
            return c

        lax.fori_loop(1, size, body, 0)

    def wait_all(axis, size, mine, src_of, dst, send, recv):
        def body(o, c):
            peer = lax.rem(mine + o, size)
            source = lax.rem(mine + size - o, size)
            remote(src_of(peer), dst.at[source], send.at[o], recv.at[o], axis, peer).wait()
            return c

        lax.fori_loop(1, size, body, 0)

    def start_chips(src_of, dst, send, recv):
        def body(o, c):
            to = lax.rem(chip + o, chips)
            remote(src_of(to), dst.at[chip], send.at[o], recv.at[o], "samp", 2 * to + core).start()
            return c

        lax.fori_loop(1, chips, body, 0)

    def wait_chips(src_of, dst, send, recv):
        def body(o, c):
            to = lax.rem(chip + o, chips)
            source = lax.rem(chip + chips - o, chips)
            remote(src_of(to), dst.at[source], send.at[o], recv.at[o], "samp", 2 * to + core).wait()
            return c

        lax.fori_loop(1, chips, body, 0)

    def one(ref):
        return lambda peer: ref

    def per_peer(ref):
        return lambda peer: ref.at[peer]

    rg_args = (one(right_ref), rg.at[core], rg_send, rg_recv)
    start_chips(*rg_args)
    rg[core, chip] = right_ref[...]
    depth = rt.shape[0] // 6
    wait_chips(*rg_args)
    across = remote(rg.at[core], rg.at[core], rh_send, rh_recv, "samp", sibling)
    across.start()
    landed = remote(rg.at[core], rg.at[1 - core], rh_send, rh_recv, "samp", sibling)
    landed.wait()
    blank = jnp.zeros((depth - right_ref.shape[0], width), jnp.float32)
    for p in range(n):
        piece = jnp.concatenate([rg[p % 2, p // 2], blank], axis=0)
        b1 = piece.astype(jnp.bfloat16)
        r1 = piece - b1.astype(jnp.float32)
        b2 = r1.astype(jnp.bfloat16)
        b3 = (r1 - b2.astype(jnp.float32)).astype(jnp.bfloat16)
        for i, part in enumerate((b1, b2, b1, b3, b2, b1)):
            rt[i * depth : (i + 1) * depth, p * width : (p + 1) * width] = part

    def build(i, c):
        geno_copy(i).wait()
        at = pl.ds(pl.multiple_of(i * ROW_STEP, ROW_STEP), ROW_STEP)
        for b in range(cols // BLOCK):
            cut = slice(b * BLOCK, (b + 1) * BLOCK)
            lowrank = dot16(lw_ref[at, :], rt[:, cut], NN)
            observed = geno[at, cut].astype(jnp.float32) - 2.0 * freqs_ref[:, cut]
            gone = mask_ref[at, b : b + 1] > 0.5
            x_ref[at, cut] = jnp.where(gone, lowrank, observed).astype(jnp.bfloat16)
        return c

    lax.fori_loop(0, steps, build, 0)

    def snp_sum(value, slots, send, recv):
        slots[my] = value
        args = ("snp", m, my, one(slots.at[my]), slots, send, recv)
        start_all(*args)

        def finish():
            wait_all(*args)
            total = slots[0].astype(jnp.float32)
            for q in range(1, m):
                total = total + slots[q].astype(jnp.float32)
            return total

        return finish

    first = dot16(x_ref[...], sketch_ref[...], NN).T.astype(jnp.bfloat16)
    y = snp_sum(first, yfirst, y_send.at[0], y_recv.at[0])()
    piece_rows = k // n
    for it in range(ITERS + 1):
        hi, lo = split2(y)
        both = jnp.concatenate([hi, lo], axis=0)
        g4 = dot16(both, both, NT)
        gram = g4[:k, :k] + (g4[:k, k:] + g4[k:, :k])
        for p in range(n):
            gr_src[it, p] = gram[p * piece_rows : (p + 1) * piece_rows]
        gr_args = ("samp", n, me, per_peer(gr_src.at[it]), gr_dst.at[it], gr_send.at[it], gr_recv.at[it])
        start_all(*gr_args)

        def sketch_half(which):
            t2 = dot16(both, x_ref[:, half_of(which)], NN)
            return t2[:k] + t2[k:]

        t = sketch_half(1 - core)
        for p in range(chips):
            t_src[it, p] = t[:, p * width : (p + 1) * width]
        across = remote(
            t_src.at[it], t_half.at[it], h_send.at[it], h_recv.at[it], "samp", sibling
        )
        across.start()
        t = sketch_half(core)
        across.wait()
        for p in range(chips):
            pair = t[:, p * width : (p + 1) * width] + t_half[it, p]
            if it == 0:
                t_sum16[p] = pair.astype(jnp.bfloat16)
            else:
                t_sum[it - 1, p] = pair
        sent = t_sum16 if it == 0 else t_sum.at[it - 1]
        arrived = t_dst16 if it == 0 else t_dst.at[it - 1]
        t_args = (per_peer(sent), arrived, t_send.at[it], t_recv.at[it])
        start_chips(*t_args)

        wait_all(*gr_args)
        gr_dst[it, me] = gr_src[it, me]
        piece = gr_dst[it, 0]
        for p in range(1, n):
            piece = piece + gr_dst[it, p]
        ga_src[it] = piece
        ga_args = ("samp", n, me, one(ga_src.at[it]), ga_dst.at[it], ga_send.at[it], ga_recv.at[it])
        start_all(*ga_args)
        ga_dst[it, me] = piece
        if it == ITERS:
            for c in range(2):
                snpb_ref[:, c * half : (c + 1) * half] = dot32(upper, zt[c].astype(jnp.float32))
        wait_all(*ga_args)
        for p in range(n):
            gfull[p * piece_rows : (p + 1) * piece_rows, :] = ga_dst[it, p]
        lower = inverse_factor(gfull[...] * (1.0 / sample_count), False)

        wait_chips(*t_args)
        arrived[chip] = sent[chip]
        chunk = arrived[0].astype(jnp.float32)
        for p in range(1, chips):
            chunk = chunk + arrived[p].astype(jnp.float32)
        z = dot32(lower, chunk)
        if it == ITERS:
            z = z * (1.0 / math.sqrt(sample_count))
        zg[it, core, chip] = z.astype(jnp.bfloat16)
        z_args = (one(zg.at[it, core, chip]), zg.at[it, core], z_send.at[it], z_recv.at[it])
        start_chips(*z_args)
        if it == ITERS:
            basis_ref[...] = dot32(lower, y)
        wait_chips(*z_args)
        across = remote(
            zg.at[it, core], zg.at[it, core], zh_send.at[it], zh_recv.at[it], "samp", sibling
        )
        across.start()
        landed = remote(
            zg.at[it, core], zg.at[it, 1 - core], zh_send.at[it], zh_recv.at[it], "samp", sibling
        )
        if it == ITERS:
            landed.wait()
            for c in range(2):
                for p in range(chips):
                    at = c * half + p * width
                    proj_ref[:, at : at + width] = zg[it, c, p].astype(jnp.float32)
            return

        def use_half(which):
            for p in range(chips):
                zt[which, :, p * width : (p + 1) * width] = zg[it, which, p]
            zz = zt[which]
            turned = zz.astype(jnp.float32).T.astype(jnp.bfloat16)
            return dot16(zz, zz, NT), dot16(x_ref[:, half_of(which)], turned, NN)

        gz_own, v_own = use_half(core)
        landed.wait()
        gz_far, v_far = use_half(1 - core)
        gz_done = snp_sum(gz_own + gz_far, gsl.at[it], gz_send.at[it], gz_recv.at[it])
        v_done = snp_sum((v_own + v_far).T, ysl.at[it], y_send.at[it + 1], y_recv.at[it + 1])
        upper = inverse_factor(gz_done() * (1.0 / snp_count), True)
        y = dot32(upper, v_done())


def on_device(
    n,
    m,
    genotype,
    freqs,
    left_factors,
    singular,
    right_factors,
    sketch,
    batch_sizes,
    missing_batch,
    missing_block,
):
    rows, cols = genotype.shape
    k = sketch.shape[1]
    rank = left_factors.shape[1]
    depth = -(-rank // 32) * 32
    width = cols // n
    batch_range = jnp.arange(BATCHES, dtype=jnp.int32)
    upto = batch_range[:, None] >= batch_range[None, :]
    ends = jnp.sum(jnp.where(upto, batch_sizes[None, :], 0), axis=1)
    begins = ends - batch_sizes
    hot = missing_batch[:, None] == batch_range[None, :]
    first = jnp.sum(jnp.where(hot, begins[None, :], 0), axis=1)
    last = jnp.sum(jnp.where(hot, ends[None, :], 0), axis=1)
    row_ids = lax.axis_index("samp") * rows + jnp.arange(rows, dtype=jnp.int32)
    inside = (row_ids[:, None] >= first[None, :]) & (row_ids[:, None] < last[None, :])
    local_block = missing_block - lax.axis_index("snp") * (cols // BLOCK)
    hot_block = local_block[:, None] == jnp.arange(128, dtype=jnp.int32)[None, :]
    mask = jnp.dot(
        inside.astype(jnp.bfloat16),
        hot_block.astype(jnp.bfloat16),
        preferred_element_type=jnp.float32,
    )

    weighted = jnp.pad(left_factors * singular[None, :], ((0, 0), (0, depth - rank)))
    a1 = lax.reduce_precision(weighted, 8, 7)
    a2 = lax.reduce_precision(weighted - a1, 8, 7)
    a3 = lax.reduce_precision(weighted - a1 - a2, 8, 7)
    lw = jnp.concatenate([a1, a1, a2, a1, a2, a3], axis=1).astype(jnp.bfloat16)
    held = -(-rank // 8) * 8
    right_t = jnp.pad(right_factors.T, ((0, held - rank), (0, 0)))

    f32, b16 = jnp.float32, jnp.bfloat16
    vm = pl.BlockSpec(memory_space=pltpu.VMEM)
    dma = pltpu.SemaphoreType.DMA
    loops = ITERS + 1
    piece = k // n
    basis_t, proj_t, snpb_t = pl.pallas_call(
        functools.partial(
            kernel,
            n,
            m,
            float(rows * n),
            float(cols * m),
        ),
        out_shape=(
            jax.ShapeDtypeStruct((k, rows), f32),
            jax.ShapeDtypeStruct((k, cols), f32),
            jax.ShapeDtypeStruct((k, cols), f32),
        ),
        in_specs=[pl.BlockSpec(memory_space=pl.ANY)] + [vm] * 5,
        out_specs=(vm, vm, vm),
        scratch_shapes=[
            pltpu.VMEM((rows, cols), jnp.int32),
            pltpu.VMEM((rows, cols), b16),
            pltpu.VMEM((2, n // 2, held, width), f32),
            pltpu.VMEM((6 * depth, cols), b16),
            pltpu.VMEM((m, k, rows), b16),
            pltpu.VMEM((ITERS, m, k, rows), f32),
            pltpu.VMEM((ITERS, m, k, k), f32),
            pltpu.VMEM((loops, n // 2, k, width), f32),
            pltpu.VMEM((loops, n // 2, k, width), f32),
            pltpu.VMEM((ITERS, n // 2, k, width), f32),
            pltpu.VMEM((ITERS, n // 2, k, width), f32),
            pltpu.VMEM((n // 2, k, width), b16),
            pltpu.VMEM((n // 2, k, width), b16),
            pltpu.VMEM((loops, n, piece, k), f32),
            pltpu.VMEM((loops, n, piece, k), f32),
            pltpu.VMEM((loops, piece, k), f32),
            pltpu.VMEM((loops, n, piece, k), f32),
            pltpu.VMEM((k, k), f32),
            pltpu.VMEM((loops, 2, n // 2, k, width), b16),
            pltpu.VMEM((2, k, cols // 2), b16),
            dma((rows // ROW_STEP,)),
            dma((n // 2,)),
            dma((n // 2,)),
            dma,
            dma,
            dma((loops, m)),
            dma((loops, m)),
            dma((ITERS, m)),
            dma((ITERS, m)),
            dma((loops,)),
            dma((loops,)),
            dma((loops, n // 2)),
            dma((loops, n // 2)),
            dma((loops,)),
            dma((loops,)),
            dma((loops, n)),
            dma((loops, n)),
            dma((loops, n)),
            dma((loops, n)),
            dma((loops, n // 2)),
            dma((loops, n // 2)),
        ],
        compiler_params=pltpu.CompilerParams(
            collective_id=0, has_side_effects=True, vmem_limit_bytes=48 * 1024 * 1024
        ),
        cost_estimate=pl.CostEstimate(
            flops=12 * rows * cols * k, bytes_accessed=4 * rows * cols, transcendentals=0
        ),
    )(genotype, freqs[None, :], lw, right_t, sketch, mask)
    return basis_t.T, proj_t.T, snpb_t.T


def solution(mesh):
    in_specs = (
        P("samp", "snp"),
        P("snp"),
        P("samp", None),
        P(),
        P(("snp", "samp"), None),
        P("snp", None),
        P(),
        P(),
        P(),
    )
    out_specs = (P("samp", None), P("snp", None), P("snp", None))
    body = functools.partial(on_device, mesh.shape["samp"], mesh.shape["snp"])
    return jax.shard_map(
        body, mesh=mesh, in_specs=in_specs, out_specs=out_specs, check_vma=False
    )
```

```python
import functools
import math

import jax
import jax.numpy as jnp
from jax import lax
from jax.experimental import pallas as pl
from jax.experimental.pallas import tpu as pltpu
from jax.sharding import PartitionSpec as P

BATCHES = 12
BLOCK = 256
ITERS = 2
MESH = pl.DeviceIdType.MESH
NT = (((1,), (1,)), ((), ()))
NN = (((1,), (0,)), ((), ()))
ROW_STEP = 128
GROUP = 8


def dot32(a, b):
    return lax.dot_general(
        a, b, NN, precision=lax.Precision.HIGHEST, preferred_element_type=jnp.float32
    )


def dot16(a, b, dims):
    return lax.dot_general(a, b, dims, preferred_element_type=jnp.float32)


def split2(v):
    hi = v.astype(jnp.bfloat16)
    lo = (v - hi.astype(jnp.float32)).astype(jnp.bfloat16)
    return hi, lo


def inverse_factor(gram, reverse):
    k = gram.shape[0]
    rows = lax.broadcasted_iota(jnp.int32, (k, 2 * k), 0)
    lanes = lax.broadcasted_iota(jnp.int32, (k, 2 * k), 1)
    unit = (lanes == rows + k).astype(jnp.float32)
    a = jnp.concatenate([gram, unit[:, k:]], axis=1)
    done = []
    for step in range(0, k, GROUP):
        count = a.shape[0]
        base = 0 if reverse else step
        local = lax.broadcasted_iota(jnp.int32, (count, 2 * k), 0)
        if reverse:
            group = [count - 1 - i for i in range(GROUP)]
        else:
            group = list(range(GROUP))
        columns = [
            jnp.broadcast_to(a[:, base + j : base + j + 1], (count, 2 * k)) for j in group
        ]
        for i in range(0, GROUP, 2):
            j1, j2 = group[i], group[i + 1]
            one, two = columns[i], columns[i + 1]
            p, q, r = one[j1 : j1 + 1, :], two[j1 : j1 + 1, :], two[j2 : j2 + 1, :]
            scale = 1.0 / (p * r - q * q)
            after = local < j2 if reverse else local > j2
            f1 = jnp.where(after, (one * r - two * q) * scale, 0.0)
            f2 = jnp.where(after, (two * p - one * q) * scale, 0.0)
            for later in range(i + 2, GROUP):
                c = columns[later]
                columns[later] = c - (f1 * c[j1 : j1 + 1, :] + f2 * c[j2 : j2 + 1, :])
            a = a - (f1 * a[j1 : j1 + 1, :] + f2 * a[j2 : j2 + 1, :])
        if reverse:
            done.insert(0, a[count - GROUP :])
            a = a[: count - GROUP]
        else:
            done.append(a[:GROUP])
            a = a[GROUP:]
    a = jnp.concatenate(done, axis=0)
    shift, near = (k - 1, rows + 1) if reverse else (1, rows - 1)
    second = lax.rem(rows, 2) == (0 if reverse else 1)
    partner = pltpu.roll(a, shift, 0)
    cross = jnp.sum(jnp.where(lanes == near, a, 0.0), axis=1, keepdims=True)
    pivot = jnp.sum(jnp.where(lanes == near, partner, 0.0), axis=1, keepdims=True)
    a = jnp.where(second, a - (cross / pivot) * partner, a)
    diag = jnp.sum(jnp.where(lanes == rows, a, 0.0), axis=1, keepdims=True)
    return a[:, k:] * lax.rsqrt(diag)


def kernel(
    n,
    m,
    sample_count,
    snp_count,
    geno_ref,
    freqs_ref,
    left_ref,
    right_ref,
    sketch_ref,
    singular_ref,
    sizes_ref,
    batch_ref,
    block_ref,
    basis_ref,
    proj_ref,
    snpb_ref,
    geno,
    freqs,
    left,
    right,
    turned_sketch,
    left_pad,
    right_pad,
    sketch,
    lw,
    mask,
    x_ref,
    rg,
    rt,
    yfirst,
    ysl,
    gsl,
    t_src,
    t_half,
    t_sum,
    t_dst,
    t_sum16,
    t_dst16,
    gr_src,
    gr_dst,
    ga_src,
    ga_dst,
    gfull,
    zg,
    zt,
    geno_sem,
    small_sem,
    rg_send,
    rg_recv,
    rh_send,
    rh_recv,
    y_send,
    y_recv,
    gz_send,
    gz_recv,
    h_send,
    h_recv,
    t_send,
    t_recv,
    zh_send,
    zh_recv,
    gr_send,
    gr_recv,
    ga_send,
    ga_recv,
    z_send,
    z_recv,
):
    me = lax.axis_index("samp")
    my = lax.axis_index("snp")
    rows, cols = x_ref.shape
    k = sketch_ref.shape[0]
    rank, depth = left_ref.shape[0], left_pad.shape[0]
    width = cols // n
    steps = rows // ROW_STEP
    chips = n // 2
    half = cols // 2
    core = lax.rem(me, 2)
    chip = me // 2
    sibling = me + 1 - 2 * core

    def half_of(which):
        return pl.ds(pl.multiple_of(which * half, half), half)

    def geno_copy(i):
        at = pl.ds(i * ROW_STEP, ROW_STEP)
        return pltpu.make_async_copy(geno_ref.at[at], geno.at[at], geno_sem.at[i])

    small = [
        pltpu.make_async_copy(src, dst, small_sem.at[i])
        for i, (src, dst) in enumerate(
            (
                (right_ref, right),
                (left_ref, left),
                (sketch_ref, turned_sketch),
                (freqs_ref, freqs),
            )
        )
    ]
    for copy in small:
        copy.start()
    for i in range(steps):
        geno_copy(i).start()

    barrier = pltpu.get_barrier_semaphore()

    def greet_samp(o, c):
        pl.semaphore_signal(
            barrier, inc=1, device_id={"samp": lax.rem(me + o, n)}, device_id_type=MESH
        )
        return c

    def greet_snp(o, c):
        pl.semaphore_signal(
            barrier, inc=1, device_id={"snp": lax.rem(my + o, m)}, device_id_type=MESH
        )
        return c

    lax.fori_loop(1, n, greet_samp, 0)
    lax.fori_loop(1, m, greet_snp, 0)
    for copy in small:
        copy.wait()
    right_pad[...] = jnp.zeros_like(right_pad)
    right_pad[:rank, :] = right[...]
    pl.semaphore_wait(barrier, n + m - 2)

    def remote(src, dst, send, recv, axis, peer):
        return pltpu.make_async_remote_copy(
            src_ref=src,
            dst_ref=dst,
            send_sem=send,
            recv_sem=recv,
            device_id={axis: peer},
            device_id_type=MESH,
        )

    def start_all(axis, size, mine, src_of, dst, send, recv):
        def body(o, c):
            peer = lax.rem(mine + o, size)
            remote(src_of(peer), dst.at[mine], send.at[o], recv.at[o], axis, peer).start()
            return c

        lax.fori_loop(1, size, body, 0)

    def wait_all(axis, size, mine, src_of, dst, send, recv):
        def body(o, c):
            peer = lax.rem(mine + o, size)
            source = lax.rem(mine + size - o, size)
            remote(src_of(peer), dst.at[source], send.at[o], recv.at[o], axis, peer).wait()
            return c

        lax.fori_loop(1, size, body, 0)

    def start_chips(src_of, dst, send, recv):
        def body(o, c):
            to = lax.rem(chip + o, chips)
            remote(src_of(to), dst.at[chip], send.at[o], recv.at[o], "samp", 2 * to + core).start()
            return c

        lax.fori_loop(1, chips, body, 0)

    def wait_chips(src_of, dst, send, recv):
        def body(o, c):
            to = lax.rem(chip + o, chips)
            source = lax.rem(chip + chips - o, chips)
            remote(src_of(to), dst.at[source], send.at[o], recv.at[o], "samp", 2 * to + core).wait()
            return c

        lax.fori_loop(1, chips, body, 0)

    def one(ref):
        return lambda peer: ref

    def per_peer(ref):
        return lambda peer: ref.at[peer]

    rg_args = (one(right_pad), rg.at[core], rg_send, rg_recv)
    start_chips(*rg_args)
    rg[core, chip] = right_pad[...]

    row_at = lax.broadcasted_iota(jnp.int32, (16, 128), 0)
    lane_at = lax.broadcasted_iota(jnp.int32, (16, 128), 1)
    first_block = my * (cols // BLOCK)
    table = jnp.zeros((16, 128), jnp.float32)
    for j in range(batch_ref.shape[0]):
        hit = (row_at == batch_ref[j]) & (lane_at == block_ref[j] - first_block)
        table = jnp.where(hit, 1.0, table)
    ids = me * rows + lax.broadcasted_iota(jnp.int32, (rows, 128), 0)
    gone_rows = jnp.zeros((rows, 128), jnp.float32)
    end = jnp.int32(0)
    for b in range(BATCHES):
        begin, end = end, end + sizes_ref[b]
        inside = (ids >= begin) & (ids < end)
        gone_rows = jnp.where(inside, table[b : b + 1, :], gone_rows)
    mask[...] = gone_rows

    left_pad[...] = jnp.zeros_like(left_pad)
    left_pad[:rank, :] = left[...]
    rank_at = lax.broadcasted_iota(jnp.int32, (depth, 128), 0)
    scales = jnp.zeros((depth, 128), jnp.float32)
    for j in range(rank):
        scales = jnp.where(rank_at == j, singular_ref[j], scales)
    weighted = left_pad[...] * scales[:, :1]
    l1 = weighted.astype(jnp.bfloat16).astype(jnp.float32)
    l2 = (weighted - l1).astype(jnp.bfloat16).astype(jnp.float32)
    l3 = weighted - l1 - l2
    lw[...] = jnp.concatenate([l1, l1, l2, l1, l2, l3], axis=0).T.astype(jnp.bfloat16)
    sketch[...] = turned_sketch[...].astype(jnp.float32).T.astype(jnp.bfloat16)
    wait_chips(*rg_args)
    across = remote(rg.at[core], rg.at[core], rh_send, rh_recv, "samp", sibling)
    across.start()
    landed = remote(rg.at[core], rg.at[1 - core], rh_send, rh_recv, "samp", sibling)
    landed.wait()
    blank = jnp.zeros((depth - right_pad.shape[0], width), jnp.float32)
    for p in range(n):
        piece = jnp.concatenate([rg[p % 2, p // 2], blank], axis=0)
        b1 = piece.astype(jnp.bfloat16)
        r1 = piece - b1.astype(jnp.float32)
        b2 = r1.astype(jnp.bfloat16)
        b3 = (r1 - b2.astype(jnp.float32)).astype(jnp.bfloat16)
        for i, part in enumerate((b1, b2, b1, b3, b2, b1)):
            rt[i * depth : (i + 1) * depth, p * width : (p + 1) * width] = part

    def build(i, c):
        geno_copy(i).wait()
        at = pl.ds(pl.multiple_of(i * ROW_STEP, ROW_STEP), ROW_STEP)
        for b in range(cols // BLOCK):
            cut = slice(b * BLOCK, (b + 1) * BLOCK)
            lowrank = dot16(lw[at, :], rt[:, cut], NN)
            observed = geno[at, cut].astype(jnp.float32) - 2.0 * freqs[:, cut]
            gone = mask[at, b : b + 1] > 0.5
            x_ref[at, cut] = jnp.where(gone, lowrank, observed).astype(jnp.bfloat16)
        return c

    lax.fori_loop(0, steps, build, 0)

    def snp_sum(value, slots, send, recv):
        slots[my] = value
        args = ("snp", m, my, one(slots.at[my]), slots, send, recv)
        start_all(*args)

        def finish():
            wait_all(*args)
            total = slots[0].astype(jnp.float32)
            for q in range(1, m):
                total = total + slots[q].astype(jnp.float32)
            return total

        return finish

    first = dot16(x_ref[...], sketch[...], NN).T.astype(jnp.bfloat16)
    y = snp_sum(first, yfirst, y_send.at[0], y_recv.at[0])()
    piece_rows = k // n
    for it in range(ITERS + 1):
        hi, lo = split2(y)
        both = jnp.concatenate([hi, lo], axis=0)
        g4 = dot16(both, both, NT)
        gram = g4[:k, :k] + (g4[:k, k:] + g4[k:, :k])
        for p in range(n):
            gr_src[it, p] = gram[p * piece_rows : (p + 1) * piece_rows]
        gr_args = ("samp", n, me, per_peer(gr_src.at[it]), gr_dst.at[it], gr_send.at[it], gr_recv.at[it])
        start_all(*gr_args)

        def sketch_half(which):
            t2 = dot16(both, x_ref[:, half_of(which)], NN)
            return t2[:k] + t2[k:]

        t = sketch_half(1 - core)
        for p in range(chips):
            t_src[it, p] = t[:, p * width : (p + 1) * width]
        across = remote(
            t_src.at[it], t_half.at[it], h_send.at[it], h_recv.at[it], "samp", sibling
        )
        across.start()
        t = sketch_half(core)
        wait_all(*gr_args)
        gr_dst[it, me] = gr_src[it, me]
        piece = gr_dst[it, 0]
        for p in range(1, n):
            piece = piece + gr_dst[it, p]
        ga_src[it] = piece
        ga_args = ("samp", n, me, one(ga_src.at[it]), ga_dst.at[it], ga_send.at[it], ga_recv.at[it])
        start_all(*ga_args)
        ga_dst[it, me] = piece
        across.wait()
        for p in range(chips):
            pair = t[:, p * width : (p + 1) * width] + t_half[it, p]
            if it == 0:
                t_sum16[p] = pair.astype(jnp.bfloat16)
            else:
                t_sum[it - 1, p] = pair
        sent = t_sum16 if it == 0 else t_sum.at[it - 1]
        arrived = t_dst16 if it == 0 else t_dst.at[it - 1]
        t_args = (per_peer(sent), arrived, t_send.at[it], t_recv.at[it])
        start_chips(*t_args)

        if it == ITERS:
            for c in range(2):
                snpb_ref[:, c * half : (c + 1) * half] = dot32(upper, zt[c].astype(jnp.float32))
        wait_all(*ga_args)
        for p in range(n):
            gfull[p * piece_rows : (p + 1) * piece_rows, :] = ga_dst[it, p]
        lower = inverse_factor(gfull[...] * (1.0 / sample_count), False)

        wait_chips(*t_args)
        arrived[chip] = sent[chip]
        chunk = arrived[0].astype(jnp.float32)
        for p in range(1, chips):
            chunk = chunk + arrived[p].astype(jnp.float32)
        z = dot32(lower, chunk)
        if it == ITERS:
            z = z * (1.0 / math.sqrt(sample_count))
        zg[it, core, chip] = z.astype(jnp.bfloat16)
        z_args = (one(zg.at[it, core, chip]), zg.at[it, core], z_send.at[it], z_recv.at[it])
        start_chips(*z_args)
        if it == ITERS:
            basis_ref[...] = dot32(lower, y)
        wait_chips(*z_args)
        across = remote(
            zg.at[it, core], zg.at[it, core], zh_send.at[it], zh_recv.at[it], "samp", sibling
        )
        across.start()
        landed = remote(
            zg.at[it, core], zg.at[it, 1 - core], zh_send.at[it], zh_recv.at[it], "samp", sibling
        )
        if it == ITERS:
            landed.wait()
            for c in range(2):
                for p in range(chips):
                    at = c * half + p * width
                    proj_ref[:, at : at + width] = zg[it, c, p].astype(jnp.float32)
            return

        def use_half(which):
            for p in range(chips):
                zt[which, :, p * width : (p + 1) * width] = zg[it, which, p]
            zz = zt[which]
            turned = zz.astype(jnp.float32).T.astype(jnp.bfloat16)
            return dot16(zz, zz, NT), dot16(x_ref[:, half_of(which)], turned, NN)

        gz_own, v_own = use_half(core)
        landed.wait()
        gz_far, v_far = use_half(1 - core)
        gz_done = snp_sum(gz_own + gz_far, gsl.at[it], gz_send.at[it], gz_recv.at[it])
        v_done = snp_sum((v_own + v_far).T, ysl.at[it], y_send.at[it + 1], y_recv.at[it + 1])
        upper = inverse_factor(gz_done() * (1.0 / snp_count), True)
        y = dot32(upper, v_done())


def on_device(
    n,
    m,
    genotype,
    freqs,
    left_factors,
    singular,
    right_factors,
    sketch,
    batch_sizes,
    missing_batch,
    missing_block,
):
    rows, cols = genotype.shape
    k = sketch.shape[1]
    rank = left_factors.shape[1]
    depth = -(-rank // 32) * 32
    width = cols // n
    held = -(-rank // 8) * 8
    f32, b16 = jnp.float32, jnp.bfloat16
    vm = pl.BlockSpec(memory_space=pltpu.VMEM)
    dma = pltpu.SemaphoreType.DMA
    loops = ITERS + 1
    piece = k // n
    basis_t, proj_t, snpb_t = pl.pallas_call(
        functools.partial(
            kernel,
            n,
            m,
            float(rows * n),
            float(cols * m),
        ),
        out_shape=(
            jax.ShapeDtypeStruct((k, rows), f32),
            jax.ShapeDtypeStruct((k, cols), f32),
            jax.ShapeDtypeStruct((k, cols), f32),
        ),
        in_specs=[pl.BlockSpec(memory_space=pl.ANY)] * 5
        + [pl.BlockSpec(memory_space=pltpu.SMEM)] * 4,
        out_specs=(vm, vm, vm),
        scratch_shapes=[
            pltpu.VMEM((rows, cols), jnp.int32),
            pltpu.VMEM((1, cols), f32),
            pltpu.VMEM((rank, rows), f32),
            pltpu.VMEM((rank, width), f32),
            pltpu.VMEM((k, cols), b16),
            pltpu.VMEM((depth, rows), f32),
            pltpu.VMEM((held, width), f32),
            pltpu.VMEM((cols, k), b16),
            pltpu.VMEM((rows, 6 * depth), b16),
            pltpu.VMEM((rows, 128), f32),
            pltpu.VMEM((rows, cols), b16),
            pltpu.VMEM((2, n // 2, held, width), f32),
            pltpu.VMEM((6 * depth, cols), b16),
            pltpu.VMEM((m, k, rows), b16),
            pltpu.VMEM((ITERS, m, k, rows), f32),
            pltpu.VMEM((ITERS, m, k, k), f32),
            pltpu.VMEM((loops, n // 2, k, width), f32),
            pltpu.VMEM((loops, n // 2, k, width), f32),
            pltpu.VMEM((ITERS, n // 2, k, width), f32),
            pltpu.VMEM((ITERS, n // 2, k, width), f32),
            pltpu.VMEM((n // 2, k, width), b16),
            pltpu.VMEM((n // 2, k, width), b16),
            pltpu.VMEM((loops, n, piece, k), f32),
            pltpu.VMEM((loops, n, piece, k), f32),
            pltpu.VMEM((loops, piece, k), f32),
            pltpu.VMEM((loops, n, piece, k), f32),
            pltpu.VMEM((k, k), f32),
            pltpu.VMEM((loops, 2, n // 2, k, width), b16),
            pltpu.VMEM((2, k, cols // 2), b16),
            dma((rows // ROW_STEP,)),
            dma((4,)),
            dma((n // 2,)),
            dma((n // 2,)),
            dma,
            dma,
            dma((loops, m)),
            dma((loops, m)),
            dma((ITERS, m)),
            dma((ITERS, m)),
            dma((loops,)),
            dma((loops,)),
            dma((loops, n // 2)),
            dma((loops, n // 2)),
            dma((loops,)),
            dma((loops,)),
            dma((loops, n)),
            dma((loops, n)),
            dma((loops, n)),
            dma((loops, n)),
            dma((loops, n // 2)),
            dma((loops, n // 2)),
        ],
        compiler_params=pltpu.CompilerParams(
            collective_id=0, has_side_effects=True, vmem_limit_bytes=48 * 1024 * 1024
        ),
        cost_estimate=pl.CostEstimate(
            flops=12 * rows * cols * k, bytes_accessed=4 * rows * cols, transcendentals=0
        ),
    )(
        genotype,
        freqs[None, :],
        left_factors.T,
        right_factors.T,
        sketch.T,
        singular,
        batch_sizes,
        missing_batch,
        missing_block,
    )
    return basis_t.T, proj_t.T, snpb_t.T


def solution(mesh):
    in_specs = (
        P("samp", "snp"),
        P("snp"),
        P("samp", None),
        P(),
        P(("snp", "samp"), None),
        P("snp", None),
        P(),
        P(),
        P(),
    )
    out_specs = (P("samp", None), P("snp", None), P("snp", None))
    body = functools.partial(on_device, mesh.shape["samp"], mesh.shape["snp"])
    return jax.shard_map(
        body, mesh=mesh, in_specs=in_specs, out_specs=out_specs, check_vma=False
    )
```

```python
import functools
import math

import jax
import jax.numpy as jnp
from jax import lax
from jax.experimental import pallas as pl
from jax.experimental.pallas import tpu as pltpu
from jax.sharding import PartitionSpec as P

BATCHES = 12
BLOCK = 256
ITERS = 2
MESH = pl.DeviceIdType.MESH
NT = (((1,), (1,)), ((), ()))
NN = (((1,), (0,)), ((), ()))
ROW_STEP = 128
GROUP = 8


def dot32(a, b):
    return lax.dot_general(
        a, b, NN, precision=lax.Precision.HIGHEST, preferred_element_type=jnp.float32
    )


def dot16(a, b, dims):
    return lax.dot_general(a, b, dims, preferred_element_type=jnp.float32)


def split2(v):
    hi = v.astype(jnp.bfloat16)
    lo = (v - hi.astype(jnp.float32)).astype(jnp.bfloat16)
    return hi, lo


def inverse_factor(gram, reverse):
    k = gram.shape[0]
    rows = lax.broadcasted_iota(jnp.int32, (k, 2 * k), 0)
    lanes = lax.broadcasted_iota(jnp.int32, (k, 2 * k), 1)
    unit = (lanes == rows + k).astype(jnp.float32)
    a = jnp.concatenate([gram, unit[:, k:]], axis=1)
    done = []
    for step in range(0, k, GROUP):
        count = a.shape[0]
        base = 0 if reverse else step
        local = lax.broadcasted_iota(jnp.int32, (count, 2 * k), 0)
        if reverse:
            group = [count - 1 - i for i in range(GROUP)]
        else:
            group = list(range(GROUP))
        columns = [
            jnp.broadcast_to(a[:, base + j : base + j + 1], (count, 2 * k)) for j in group
        ]
        for i in range(0, GROUP, 2):
            j1, j2 = group[i], group[i + 1]
            one, two = columns[i], columns[i + 1]
            p, q, r = one[j1 : j1 + 1, :], two[j1 : j1 + 1, :], two[j2 : j2 + 1, :]
            scale = 1.0 / (p * r - q * q)
            after = local < j2 if reverse else local > j2
            f1 = jnp.where(after, (one * r - two * q) * scale, 0.0)
            f2 = jnp.where(after, (two * p - one * q) * scale, 0.0)
            for later in range(i + 2, GROUP):
                c = columns[later]
                columns[later] = c - (f1 * c[j1 : j1 + 1, :] + f2 * c[j2 : j2 + 1, :])
            a = a - (f1 * a[j1 : j1 + 1, :] + f2 * a[j2 : j2 + 1, :])
        if reverse:
            done.insert(0, a[count - GROUP :])
            a = a[: count - GROUP]
        else:
            done.append(a[:GROUP])
            a = a[GROUP:]
    a = jnp.concatenate(done, axis=0)
    shift, near = (k - 1, rows + 1) if reverse else (1, rows - 1)
    second = lax.rem(rows, 2) == (0 if reverse else 1)
    partner = pltpu.roll(a, shift, 0)
    cross = jnp.sum(jnp.where(lanes == near, a, 0.0), axis=1, keepdims=True)
    pivot = jnp.sum(jnp.where(lanes == near, partner, 0.0), axis=1, keepdims=True)
    a = jnp.where(second, a - (cross / pivot) * partner, a)
    diag = jnp.sum(jnp.where(lanes == rows, a, 0.0), axis=1, keepdims=True)
    return a[:, k:] * lax.rsqrt(diag)


def kernel(
    n,
    m,
    sample_count,
    snp_count,
    geno_ref,
    freqs_ref,
    left_ref,
    right_ref,
    sketch_ref,
    singular_any,
    sizes_any,
    batch_any,
    block_any,
    basis_ref,
    proj_ref,
    snpb_ref,
    geno,
    singular_ref,
    sizes_ref,
    batch_ref,
    block_ref,
    freqs,
    left,
    right,
    turned_sketch,
    left_pad,
    right_pad,
    sketch,
    lw,
    mask,
    x_ref,
    rg,
    rt,
    yfirst,
    ysl,
    gsl,
    t_src,
    t_half,
    t_sum,
    t_dst,
    t_sum16,
    t_dst16,
    g_src,
    g_half,
    g_all,
    zg,
    zt,
    geno_sem,
    small_sem,
    rg_send,
    rg_recv,
    rh_send,
    rh_recv,
    y_send,
    y_recv,
    gz_send,
    gz_recv,
    h_send,
    h_recv,
    t_send,
    t_recv,
    zh_send,
    zh_recv,
    gh_send,
    gh_recv,
    ga_send,
    ga_recv,
    z_send,
    z_recv,
):
    me = lax.axis_index("samp")
    my = lax.axis_index("snp")
    rows, cols = x_ref.shape
    k = sketch_ref.shape[0]
    rank, depth = left_ref.shape[0], left_pad.shape[0]
    width = cols // n
    steps = rows // ROW_STEP
    chips = n // 2
    half = cols // 2
    core = lax.rem(me, 2)
    chip = me // 2
    sibling = me + 1 - 2 * core

    def half_of(which):
        return pl.ds(pl.multiple_of(which * half, half), half)

    def geno_copy(i):
        at = pl.ds(i * ROW_STEP, ROW_STEP)
        return pltpu.make_async_copy(geno_ref.at[at], geno.at[at], geno_sem.at[i])

    small = [
        pltpu.make_async_copy(src, dst, small_sem.at[i])
        for i, (src, dst) in enumerate(
            (
                (right_ref, right),
                (left_ref, left),
                (sketch_ref, turned_sketch),
                (freqs_ref, freqs),
                (singular_any, singular_ref),
                (sizes_any, sizes_ref),
                (batch_any, batch_ref),
                (block_any, block_ref),
            )
        )
    ]
    for copy in small:
        copy.start()
    for i in range(steps):
        geno_copy(i).start()

    barrier = pltpu.get_barrier_semaphore()

    def greet_samp(o, c):
        pl.semaphore_signal(
            barrier, inc=1, device_id={"samp": lax.rem(me + o, n)}, device_id_type=MESH
        )
        return c

    def greet_snp(o, c):
        pl.semaphore_signal(
            barrier, inc=1, device_id={"snp": lax.rem(my + o, m)}, device_id_type=MESH
        )
        return c

    lax.fori_loop(1, n, greet_samp, 0)
    lax.fori_loop(1, m, greet_snp, 0)
    for copy in small:
        copy.wait()
    right_pad[...] = jnp.zeros_like(right_pad)
    right_pad[:rank, :] = right[...]
    pl.semaphore_wait(barrier, n + m - 2)

    def remote(src, dst, send, recv, axis, peer):
        return pltpu.make_async_remote_copy(
            src_ref=src,
            dst_ref=dst,
            send_sem=send,
            recv_sem=recv,
            device_id={axis: peer},
            device_id_type=MESH,
        )

    def start_all(axis, size, mine, src_of, dst, send, recv):
        def body(o, c):
            peer = lax.rem(mine + o, size)
            remote(src_of(peer), dst.at[mine], send.at[o], recv.at[o], axis, peer).start()
            return c

        lax.fori_loop(1, size, body, 0)

    def wait_all(axis, size, mine, src_of, dst, send, recv):
        def body(o, c):
            peer = lax.rem(mine + o, size)
            source = lax.rem(mine + size - o, size)
            remote(src_of(peer), dst.at[source], send.at[o], recv.at[o], axis, peer).wait()
            return c

        lax.fori_loop(1, size, body, 0)

    def start_chips(src_of, dst, send, recv):
        def body(o, c):
            to = lax.rem(chip + o, chips)
            remote(src_of(to), dst.at[chip], send.at[o], recv.at[o], "samp", 2 * to + core).start()
            return c

        lax.fori_loop(1, chips, body, 0)

    def wait_chips(src_of, dst, send, recv):
        def body(o, c):
            to = lax.rem(chip + o, chips)
            source = lax.rem(chip + chips - o, chips)
            remote(src_of(to), dst.at[source], send.at[o], recv.at[o], "samp", 2 * to + core).wait()
            return c

        lax.fori_loop(1, chips, body, 0)

    def one(ref):
        return lambda peer: ref

    def per_peer(ref):
        return lambda peer: ref.at[peer]

    rg_args = (one(right_pad), rg.at[core], rg_send, rg_recv)
    start_chips(*rg_args)
    rg[core, chip] = right_pad[...]

    row_at = lax.broadcasted_iota(jnp.int32, (16, 128), 0)
    lane_at = lax.broadcasted_iota(jnp.int32, (16, 128), 1)
    first_block = my * (cols // BLOCK)
    table = jnp.zeros((16, 128), jnp.float32)
    for j in range(batch_ref.shape[0]):
        hit = (row_at == batch_ref[j]) & (lane_at == block_ref[j] - first_block)
        table = jnp.where(hit, 1.0, table)
    ids = me * rows + lax.broadcasted_iota(jnp.int32, (rows, 128), 0)
    gone_rows = jnp.zeros((rows, 128), jnp.float32)
    end = jnp.int32(0)
    for b in range(BATCHES):
        begin, end = end, end + sizes_ref[b]
        inside = (ids >= begin) & (ids < end)
        gone_rows = jnp.where(inside, table[b : b + 1, :], gone_rows)
    mask[...] = gone_rows

    left_pad[...] = jnp.zeros_like(left_pad)
    left_pad[:rank, :] = left[...]
    rank_at = lax.broadcasted_iota(jnp.int32, (depth, 128), 0)
    scales = jnp.zeros((depth, 128), jnp.float32)
    for j in range(rank):
        scales = jnp.where(rank_at == j, singular_ref[j], scales)
    weighted = left_pad[...] * scales[:, :1]
    l1 = weighted.astype(jnp.bfloat16).astype(jnp.float32)
    l2 = (weighted - l1).astype(jnp.bfloat16).astype(jnp.float32)
    l3 = weighted - l1 - l2
    lw[...] = jnp.concatenate([l1, l1, l2, l1, l2, l3], axis=0).T.astype(jnp.bfloat16)
    sketch[...] = turned_sketch[...].astype(jnp.float32).T.astype(jnp.bfloat16)
    wait_chips(*rg_args)
    across = remote(rg.at[core], rg.at[core], rh_send, rh_recv, "samp", sibling)
    across.start()
    landed = remote(rg.at[core], rg.at[1 - core], rh_send, rh_recv, "samp", sibling)
    landed.wait()
    blank = jnp.zeros((depth - right_pad.shape[0], width), jnp.float32)
    for p in range(n):
        piece = jnp.concatenate([rg[p % 2, p // 2], blank], axis=0)
        b1 = piece.astype(jnp.bfloat16)
        r1 = piece - b1.astype(jnp.float32)
        b2 = r1.astype(jnp.bfloat16)
        b3 = (r1 - b2.astype(jnp.float32)).astype(jnp.bfloat16)
        for i, part in enumerate((b1, b2, b1, b3, b2, b1)):
            rt[i * depth : (i + 1) * depth, p * width : (p + 1) * width] = part

    def build(i, c):
        geno_copy(i).wait()
        at = pl.ds(pl.multiple_of(i * ROW_STEP, ROW_STEP), ROW_STEP)
        for b in range(cols // BLOCK):
            cut = slice(b * BLOCK, (b + 1) * BLOCK)
            lowrank = dot16(lw[at, :], rt[:, cut], NN)
            observed = geno[at, cut].astype(jnp.float32) - 2.0 * freqs[:, cut]
            gone = mask[at, b : b + 1] > 0.5
            x_ref[at, cut] = jnp.where(gone, lowrank, observed).astype(jnp.bfloat16)
        return c

    lax.fori_loop(0, steps, build, 0)

    def snp_sum(value, slots, send, recv):
        slots[my] = value
        args = ("snp", m, my, one(slots.at[my]), slots, send, recv)
        start_all(*args)

        def finish():
            wait_all(*args)
            total = slots[0].astype(jnp.float32)
            for q in range(1, m):
                total = total + slots[q].astype(jnp.float32)
            return total

        return finish

    first = dot16(x_ref[...], sketch[...], NN).T.astype(jnp.bfloat16)
    y = snp_sum(first, yfirst, y_send.at[0], y_recv.at[0])()
    for it in range(ITERS + 1):
        hi, lo = split2(y)
        both = jnp.concatenate([hi, lo], axis=0)
        g4 = dot16(both, both, NT)
        gram = g4[:k, :k] + (g4[:k, k:] + g4[k:, :k])
        g_src[it] = jnp.concatenate([gram[: k // 2], gram[k // 2 :]], axis=1)
        g_across = remote(
            g_src.at[it], g_half.at[it], gh_send.at[it], gh_recv.at[it], "samp", sibling
        )
        g_across.start()

        def sketch_half(which):
            t2 = dot16(both, x_ref[:, half_of(which)], NN)
            return t2[:k] + t2[k:]

        t = sketch_half(1 - core)
        for p in range(chips):
            t_src[it, p] = t[:, p * width : (p + 1) * width]
        across = remote(
            t_src.at[it], t_half.at[it], h_send.at[it], h_recv.at[it], "samp", sibling
        )
        across.start()
        g_across.wait()
        g_all[it, chip] = g_src[it] + g_half[it]
        g_args = (one(g_all.at[it, chip]), g_all.at[it], ga_send.at[it], ga_recv.at[it])
        start_chips(*g_args)
        t = sketch_half(core)
        across.wait()
        for p in range(chips):
            pair = t[:, p * width : (p + 1) * width] + t_half[it, p]
            if it == 0:
                t_sum16[p] = pair.astype(jnp.bfloat16)
            else:
                t_sum[it - 1, p] = pair
        sent = t_sum16 if it == 0 else t_sum.at[it - 1]
        arrived = t_dst16 if it == 0 else t_dst.at[it - 1]
        t_args = (per_peer(sent), arrived, t_send.at[it], t_recv.at[it])
        start_chips(*t_args)

        if it == ITERS:
            for c in range(2):
                snpb_ref[:, c * half : (c + 1) * half] = dot32(upper, zt[c].astype(jnp.float32))
        wait_chips(*g_args)
        packed = g_all[it, 0]
        for p in range(1, chips):
            packed = packed + g_all[it, p]
        gram = jnp.concatenate([packed[:, :k], packed[:, k:]], axis=0)
        lower = inverse_factor(gram * (1.0 / sample_count), False)

        wait_chips(*t_args)
        arrived[chip] = sent[chip]
        chunk = arrived[0].astype(jnp.float32)
        for p in range(1, chips):
            chunk = chunk + arrived[p].astype(jnp.float32)
        z = dot32(lower, chunk)
        if it == ITERS:
            z = z * (1.0 / math.sqrt(sample_count))
        zg[it, core, chip] = z.astype(jnp.bfloat16)
        z_args = (one(zg.at[it, core, chip]), zg.at[it, core], z_send.at[it], z_recv.at[it])
        start_chips(*z_args)
        if it == ITERS:
            basis_ref[...] = dot32(lower, y)
        wait_chips(*z_args)
        across = remote(
            zg.at[it, core], zg.at[it, core], zh_send.at[it], zh_recv.at[it], "samp", sibling
        )
        across.start()
        landed = remote(
            zg.at[it, core], zg.at[it, 1 - core], zh_send.at[it], zh_recv.at[it], "samp", sibling
        )
        if it == ITERS:
            landed.wait()
            for c in range(2):
                for p in range(chips):
                    at = c * half + p * width
                    proj_ref[:, at : at + width] = zg[it, c, p].astype(jnp.float32)
            return

        def use_half(which):
            for p in range(chips):
                zt[which, :, p * width : (p + 1) * width] = zg[it, which, p]
            zz = zt[which]
            turned = zz.astype(jnp.float32).T.astype(jnp.bfloat16)
            return dot16(zz, zz, NT), dot16(x_ref[:, half_of(which)], turned, NN)

        gz_own, v_own = use_half(core)
        landed.wait()
        gz_far, v_far = use_half(1 - core)
        gz_done = snp_sum(gz_own + gz_far, gsl.at[it], gz_send.at[it], gz_recv.at[it])
        v_done = snp_sum((v_own + v_far).T, ysl.at[it], y_send.at[it + 1], y_recv.at[it + 1])
        upper = inverse_factor(gz_done() * (1.0 / snp_count), True)
        y = dot32(upper, v_done())


def on_device(
    n,
    m,
    genotype,
    freqs,
    left_factors,
    singular,
    right_factors,
    sketch,
    batch_sizes,
    missing_batch,
    missing_block,
):
    rows, cols = genotype.shape
    k = sketch.shape[1]
    rank = left_factors.shape[1]
    depth = -(-rank // 32) * 32
    width = cols // n
    held = -(-rank // 8) * 8
    f32, b16 = jnp.float32, jnp.bfloat16
    vm = pl.BlockSpec(memory_space=pltpu.VMEM)
    dma = pltpu.SemaphoreType.DMA
    loops = ITERS + 1
    basis_t, proj_t, snpb_t = pl.pallas_call(
        functools.partial(
            kernel,
            n,
            m,
            float(rows * n),
            float(cols * m),
        ),
        out_shape=(
            jax.ShapeDtypeStruct((k, rows), f32),
            jax.ShapeDtypeStruct((k, cols), f32),
            jax.ShapeDtypeStruct((k, cols), f32),
        ),
        in_specs=[pl.BlockSpec(memory_space=pl.ANY)] * 9,
        out_specs=(vm, vm, vm),
        scratch_shapes=[
            pltpu.VMEM((rows, cols), jnp.int32),
            pltpu.SMEM(singular.shape, f32),
            pltpu.SMEM(batch_sizes.shape, jnp.int32),
            pltpu.SMEM(missing_batch.shape, jnp.int32),
            pltpu.SMEM(missing_block.shape, jnp.int32),
            pltpu.VMEM((1, cols), f32),
            pltpu.VMEM((rank, rows), f32),
            pltpu.VMEM((rank, width), f32),
            pltpu.VMEM((k, cols), b16),
            pltpu.VMEM((depth, rows), f32),
            pltpu.VMEM((held, width), f32),
            pltpu.VMEM((cols, k), b16),
            pltpu.VMEM((rows, 6 * depth), b16),
            pltpu.VMEM((rows, 128), f32),
            pltpu.VMEM((rows, cols), b16),
            pltpu.VMEM((2, n // 2, held, width), f32),
            pltpu.VMEM((6 * depth, cols), b16),
            pltpu.VMEM((m, k, rows), b16),
            pltpu.VMEM((ITERS, m, k, rows), f32),
            pltpu.VMEM((ITERS, m, k, k), f32),
            pltpu.VMEM((loops, n // 2, k, width), f32),
            pltpu.VMEM((loops, n // 2, k, width), f32),
            pltpu.VMEM((ITERS, n // 2, k, width), f32),
            pltpu.VMEM((ITERS, n // 2, k, width), f32),
            pltpu.VMEM((n // 2, k, width), b16),
            pltpu.VMEM((n // 2, k, width), b16),
            pltpu.VMEM((loops, k // 2, 2 * k), f32),
            pltpu.VMEM((loops, k // 2, 2 * k), f32),
            pltpu.VMEM((loops, n // 2, k // 2, 2 * k), f32),
            pltpu.VMEM((loops, 2, n // 2, k, width), b16),
            pltpu.VMEM((2, k, cols // 2), b16),
            dma((rows // ROW_STEP,)),
            dma((8,)),
            dma((n // 2,)),
            dma((n // 2,)),
            dma,
            dma,
            dma((loops, m)),
            dma((loops, m)),
            dma((ITERS, m)),
            dma((ITERS, m)),
            dma((loops,)),
            dma((loops,)),
            dma((loops, n // 2)),
            dma((loops, n // 2)),
            dma((loops,)),
            dma((loops,)),
            dma((loops,)),
            dma((loops,)),
            dma((loops, n // 2)),
            dma((loops, n // 2)),
            dma((loops, n // 2)),
            dma((loops, n // 2)),
        ],
        compiler_params=pltpu.CompilerParams(
            collective_id=0, has_side_effects=True, vmem_limit_bytes=62 * 1024 * 1024
        ),
        cost_estimate=pl.CostEstimate(
            flops=12 * rows * cols * k, bytes_accessed=4 * rows * cols, transcendentals=0
        ),
    )(
        genotype,
        freqs[None, :],
        left_factors.T,
        right_factors.T,
        sketch.T,
        singular,
        batch_sizes,
        missing_batch,
        missing_block,
    )
    return basis_t.T, proj_t.T, snpb_t.T


def solution(mesh):
    in_specs = (
        P("samp", "snp"),
        P("snp"),
        P("samp", None),
        P(),
        P(("snp", "samp"), None),
        P("snp", None),
        P(),
        P(),
        P(),
    )
    out_specs = (P("samp", None), P("snp", None), P("snp", None))
    body = functools.partial(on_device, mesh.shape["samp"], mesh.shape["snp"])
    return jax.shard_map(
        body, mesh=mesh, in_specs=in_specs, out_specs=out_specs, check_vma=False
    )
```

```python
import functools
import math

import jax
import jax.numpy as jnp
from jax import lax
from jax.experimental import pallas as pl
from jax.experimental.pallas import tpu as pltpu
from jax.sharding import PartitionSpec as P

BATCHES = 12
BLOCK = 256
ITERS = 2
MESH = pl.DeviceIdType.MESH
NT = (((1,), (1,)), ((), ()))
NN = (((1,), (0,)), ((), ()))
ROW_STEP = 128
GROUP = 8


def dot32(a, b):
    return lax.dot_general(
        a, b, NN, precision=lax.Precision.HIGHEST, preferred_element_type=jnp.float32
    )


def dot16(a, b, dims):
    return lax.dot_general(a, b, dims, preferred_element_type=jnp.float32)


def split2(v):
    hi = v.astype(jnp.bfloat16)
    lo = (v - hi.astype(jnp.float32)).astype(jnp.bfloat16)
    return hi, lo


def inverse_factor(gram, reverse):
    k = gram.shape[0]
    rows = lax.broadcasted_iota(jnp.int32, (k, 2 * k), 0)
    lanes = lax.broadcasted_iota(jnp.int32, (k, 2 * k), 1)
    unit = (lanes == rows + k).astype(jnp.float32)
    a = jnp.concatenate([gram, unit[:, k:]], axis=1)
    done = []
    for step in range(0, k, GROUP):
        count = a.shape[0]
        base = 0 if reverse else step
        local = lax.broadcasted_iota(jnp.int32, (count, 2 * k), 0)
        if reverse:
            group = [count - 1 - i for i in range(GROUP)]
        else:
            group = list(range(GROUP))
        columns = [
            jnp.broadcast_to(a[:, base + j : base + j + 1], (count, 2 * k)) for j in group
        ]
        for i in range(0, GROUP, 2):
            j1, j2 = group[i], group[i + 1]
            one, two = columns[i], columns[i + 1]
            p, q, r = one[j1 : j1 + 1, :], two[j1 : j1 + 1, :], two[j2 : j2 + 1, :]
            scale = 1.0 / (p * r - q * q)
            after = local < j2 if reverse else local > j2
            f1 = jnp.where(after, (one * r - two * q) * scale, 0.0)
            f2 = jnp.where(after, (two * p - one * q) * scale, 0.0)
            for later in range(i + 2, GROUP):
                c = columns[later]
                columns[later] = c - (f1 * c[j1 : j1 + 1, :] + f2 * c[j2 : j2 + 1, :])
            a = a - (f1 * a[j1 : j1 + 1, :] + f2 * a[j2 : j2 + 1, :])
        if reverse:
            done.insert(0, a[count - GROUP :])
            a = a[: count - GROUP]
        else:
            done.append(a[:GROUP])
            a = a[GROUP:]
    a = jnp.concatenate(done, axis=0)
    shift, near = (k - 1, rows + 1) if reverse else (1, rows - 1)
    second = lax.rem(rows, 2) == (0 if reverse else 1)
    partner = pltpu.roll(a, shift, 0)
    cross = jnp.sum(jnp.where(lanes == near, a, 0.0), axis=1, keepdims=True)
    pivot = jnp.sum(jnp.where(lanes == near, partner, 0.0), axis=1, keepdims=True)
    a = jnp.where(second, a - (cross / pivot) * partner, a)
    diag = jnp.sum(jnp.where(lanes == rows, a, 0.0), axis=1, keepdims=True)
    return a[:, k:] * lax.rsqrt(diag)


def kernel(
    n,
    m,
    sample_count,
    snp_count,
    geno_ref,
    freqs_ref,
    left_ref,
    right_ref,
    sketch_ref,
    singular_any,
    sizes_any,
    batch_any,
    block_any,
    basis_ref,
    proj_ref,
    snpb_ref,
    geno,
    singular_ref,
    sizes_ref,
    batch_ref,
    block_ref,
    freqs,
    left,
    right,
    turned_sketch,
    left_pad,
    right_pad,
    sketch,
    lw,
    mask,
    x_ref,
    rg,
    rt,
    yfirst,
    ysl,
    gsl,
    t_src,
    t_half,
    t_sum,
    t_dst,
    t_sum16,
    t_dst16,
    g_src,
    g_half,
    g_all,
    zg,
    zt,
    geno_sem,
    small_sem,
    rg_send,
    rg_recv,
    rh_send,
    rh_recv,
    y_send,
    y_recv,
    gz_send,
    gz_recv,
    h_send,
    h_recv,
    t_send,
    t_recv,
    zh_send,
    zh_recv,
    gh_send,
    gh_recv,
    ga_send,
    ga_recv,
    z_send,
    z_recv,
):
    me = lax.axis_index("samp")
    my = lax.axis_index("snp")
    rows, cols = x_ref.shape
    k = sketch_ref.shape[0]
    rank, depth = left_ref.shape[0], left_pad.shape[0]
    width = cols // n
    steps = rows // ROW_STEP
    chips = n // 2
    half = cols // 2
    core = lax.rem(me, 2)
    chip = me // 2
    sibling = me + 1 - 2 * core

    def half_of(which):
        return pl.ds(pl.multiple_of(which * half, half), half)

    def geno_copy(i):
        at = pl.ds(i * ROW_STEP, ROW_STEP)
        return pltpu.make_async_copy(geno_ref.at[at], geno.at[at], geno_sem.at[i])

    small = [
        pltpu.make_async_copy(src, dst, small_sem.at[i])
        for i, (src, dst) in enumerate(
            (
                (right_ref, right),
                (left_ref, left),
                (sketch_ref, turned_sketch),
                (freqs_ref, freqs),
                (singular_any, singular_ref),
                (sizes_any, sizes_ref),
                (batch_any, batch_ref),
                (block_any, block_ref),
            )
        )
    ]
    for copy in small:
        copy.start()
    for i in range(steps):
        geno_copy(i).start()

    barrier = pltpu.get_barrier_semaphore()

    def greet_samp(o, c):
        pl.semaphore_signal(
            barrier, inc=1, device_id={"samp": lax.rem(me + o, n)}, device_id_type=MESH
        )
        return c

    def greet_snp(o, c):
        pl.semaphore_signal(
            barrier, inc=1, device_id={"snp": lax.rem(my + o, m)}, device_id_type=MESH
        )
        return c

    lax.fori_loop(1, n, greet_samp, 0)
    lax.fori_loop(1, m, greet_snp, 0)
    for copy in small:
        copy.wait()
    right_pad[...] = jnp.zeros_like(right_pad)
    right_pad[:rank, :] = right[...]
    pl.semaphore_wait(barrier, n + m - 2)

    def remote(src, dst, send, recv, axis, peer):
        return pltpu.make_async_remote_copy(
            src_ref=src,
            dst_ref=dst,
            send_sem=send,
            recv_sem=recv,
            device_id={axis: peer},
            device_id_type=MESH,
        )

    def start_all(axis, size, mine, src_of, dst, send, recv):
        def body(o, c):
            peer = lax.rem(mine + o, size)
            remote(src_of(peer), dst.at[mine], send.at[o], recv.at[o], axis, peer).start()
            return c

        lax.fori_loop(1, size, body, 0)

    def wait_all(axis, size, mine, src_of, dst, send, recv):
        def body(o, c):
            peer = lax.rem(mine + o, size)
            source = lax.rem(mine + size - o, size)
            remote(src_of(peer), dst.at[source], send.at[o], recv.at[o], axis, peer).wait()
            return c

        lax.fori_loop(1, size, body, 0)

    def start_chips(src_of, dst, send, recv):
        def body(o, c):
            to = lax.rem(chip + o, chips)
            remote(src_of(to), dst.at[chip], send.at[o], recv.at[o], "samp", 2 * to + core).start()
            return c

        lax.fori_loop(1, chips, body, 0)

    def wait_chips(src_of, dst, send, recv):
        def body(o, c):
            to = lax.rem(chip + o, chips)
            source = lax.rem(chip + chips - o, chips)
            remote(src_of(to), dst.at[source], send.at[o], recv.at[o], "samp", 2 * to + core).wait()
            return c

        lax.fori_loop(1, chips, body, 0)

    def one(ref):
        return lambda peer: ref

    def per_peer(ref):
        return lambda peer: ref.at[peer]

    rg_args = (one(right_pad), rg.at[core], rg_send, rg_recv)
    start_chips(*rg_args)
    rg[core, chip] = right_pad[...]

    row_at = lax.broadcasted_iota(jnp.int32, (16, 128), 0)
    lane_at = lax.broadcasted_iota(jnp.int32, (16, 128), 1)
    first_block = my * (cols // BLOCK)
    table = jnp.zeros((16, 128), jnp.float32)
    for j in range(batch_ref.shape[0]):
        hit = (row_at == batch_ref[j]) & (lane_at == block_ref[j] - first_block)
        table = jnp.where(hit, 1.0, table)
    ids = me * rows + lax.broadcasted_iota(jnp.int32, (rows, 128), 0)
    gone_rows = jnp.zeros((rows, 128), jnp.float32)
    end = jnp.int32(0)
    for b in range(BATCHES):
        begin, end = end, end + sizes_ref[b]
        inside = (ids >= begin) & (ids < end)
        gone_rows = jnp.where(inside, table[b : b + 1, :], gone_rows)
    mask[...] = gone_rows

    left_pad[...] = jnp.zeros_like(left_pad)
    left_pad[:rank, :] = left[...]
    rank_at = lax.broadcasted_iota(jnp.int32, (depth, 128), 0)
    scales = jnp.zeros((depth, 128), jnp.float32)
    for j in range(rank):
        scales = jnp.where(rank_at == j, singular_ref[j], scales)
    weighted = left_pad[...] * scales[:, :1]
    l1 = weighted.astype(jnp.bfloat16).astype(jnp.float32)
    l2 = (weighted - l1).astype(jnp.bfloat16).astype(jnp.float32)
    l3 = weighted - l1 - l2
    lw[...] = jnp.concatenate([l1, l1, l2, l1, l2, l3], axis=0).T.astype(jnp.bfloat16)
    sketch[...] = turned_sketch[...].astype(jnp.float32).T.astype(jnp.bfloat16)
    wait_chips(*rg_args)
    across = remote(rg.at[core], rg.at[core], rh_send, rh_recv, "samp", sibling)
    across.start()
    landed = remote(rg.at[core], rg.at[1 - core], rh_send, rh_recv, "samp", sibling)
    landed.wait()
    blank = jnp.zeros((depth - right_pad.shape[0], width), jnp.float32)
    for p in range(n):
        piece = jnp.concatenate([rg[p % 2, p // 2], blank], axis=0)
        b1 = piece.astype(jnp.bfloat16)
        r1 = piece - b1.astype(jnp.float32)
        b2 = r1.astype(jnp.bfloat16)
        b3 = (r1 - b2.astype(jnp.float32)).astype(jnp.bfloat16)
        for i, part in enumerate((b1, b2, b1, b3, b2, b1)):
            rt[i * depth : (i + 1) * depth, p * width : (p + 1) * width] = part

    def build(i, c):
        geno_copy(i).wait()
        at = pl.ds(pl.multiple_of(i * ROW_STEP, ROW_STEP), ROW_STEP)
        for b in range(cols // BLOCK):
            cut = slice(b * BLOCK, (b + 1) * BLOCK)
            lowrank = dot16(lw[at, :], rt[:, cut], NN)
            observed = geno[at, cut].astype(jnp.float32) - 2.0 * freqs[:, cut]
            gone = mask[at, b : b + 1] > 0.5
            x_ref[at, cut] = jnp.where(gone, lowrank, observed).astype(jnp.bfloat16)
        return c

    lax.fori_loop(0, steps, build, 0)

    def snp_sum(value, slots, send, recv):
        slots[my] = value
        args = ("snp", m, my, one(slots.at[my]), slots, send, recv)
        start_all(*args)

        def finish():
            wait_all(*args)
            total = slots[0].astype(jnp.float32)
            for q in range(1, m):
                total = total + slots[q].astype(jnp.float32)
            return total

        return finish

    first = dot16(x_ref[...], sketch[...], NN).T.astype(jnp.bfloat16)
    y = snp_sum(first, yfirst, y_send.at[0], y_recv.at[0])()
    for it in range(ITERS + 1):
        hi, lo = split2(y)
        both = jnp.concatenate([hi, lo], axis=0)
        g4 = dot16(both, both, NT)
        gram = g4[:k, :k] + (g4[:k, k:] + g4[k:, :k])
        g_src[it] = jnp.concatenate([gram[: k // 2], gram[k // 2 :]], axis=1)
        g_across = remote(
            g_src.at[it], g_half.at[it], gh_send.at[it], gh_recv.at[it], "samp", sibling
        )
        g_across.start()

        def sketch_half(which):
            t2 = dot16(both, x_ref[:, half_of(which)], NN)
            return t2[:k] + t2[k:]

        t = sketch_half(1 - core)
        for p in range(chips):
            t_src[it, p] = t[:, p * width : (p + 1) * width]
        across = remote(
            t_src.at[it], t_half.at[it], h_send.at[it], h_recv.at[it], "samp", sibling
        )
        across.start()
        g_across.wait()
        g_all[it, chip] = g_src[it] + g_half[it]
        g_args = (one(g_all.at[it, chip]), g_all.at[it], ga_send.at[it], ga_recv.at[it])
        start_chips(*g_args)
        t = sketch_half(core)
        across.wait()
        for p in range(chips):
            pair = t[:, p * width : (p + 1) * width] + t_half[it, p]
            if it == 0:
                t_sum16[p] = pair.astype(jnp.bfloat16)
            else:
                t_sum[it - 1, p] = pair
        sent = t_sum16 if it == 0 else t_sum.at[it - 1]
        arrived = t_dst16 if it == 0 else t_dst.at[it - 1]
        t_args = (per_peer(sent), arrived, t_send.at[it], t_recv.at[it])
        start_chips(*t_args)

        if it == ITERS:
            for c in range(2):
                snpb_ref[:, c * half : (c + 1) * half] = dot32(upper, zt[c].astype(jnp.float32))
        wait_chips(*g_args)
        packed = g_all[it, 0]
        for p in range(1, chips):
            packed = packed + g_all[it, p]
        gram = jnp.concatenate([packed[:, :k], packed[:, k:]], axis=0)
        lower = inverse_factor(gram * (1.0 / sample_count), False)

        wait_chips(*t_args)
        arrived[chip] = sent[chip]
        chunk = arrived[0].astype(jnp.float32)
        for p in range(1, chips):
            chunk = chunk + arrived[p].astype(jnp.float32)
        z = dot32(lower, chunk)
        if it == ITERS:
            z = z * (1.0 / math.sqrt(sample_count))
        zg[it, core, chip] = z.astype(jnp.bfloat16)
        z_args = (one(zg.at[it, core, chip]), zg.at[it, core], z_send.at[it], z_recv.at[it])
        start_chips(*z_args)
        if it == ITERS:
            basis_ref[...] = dot32(lower, y)
        wait_chips(*z_args)
        across = remote(
            zg.at[it, core], zg.at[it, core], zh_send.at[it], zh_recv.at[it], "samp", sibling
        )
        across.start()
        landed = remote(
            zg.at[it, core], zg.at[it, 1 - core], zh_send.at[it], zh_recv.at[it], "samp", sibling
        )
        if it == ITERS:
            landed.wait()
            for c in range(2):
                for p in range(chips):
                    at = c * half + p * width
                    proj_ref[:, at : at + width] = zg[it, c, p].astype(jnp.float32)
            return

        def use_half(which):
            for p in range(chips):
                zt[which, :, p * width : (p + 1) * width] = zg[it, which, p]
            zz = zt[which]
            turned = zz.astype(jnp.float32).T.astype(jnp.bfloat16)
            return dot16(zz, zz, NT), dot16(x_ref[:, half_of(which)], turned, NN)

        gz_own, v_own = use_half(core)
        landed.wait()
        gz_far, v_far = use_half(1 - core)
        gz_done = snp_sum(gz_own + gz_far, gsl.at[it], gz_send.at[it], gz_recv.at[it])
        v_done = snp_sum((v_own + v_far).T, ysl.at[it], y_send.at[it + 1], y_recv.at[it + 1])
        upper = inverse_factor(gz_done() * (1.0 / snp_count), True)
        y = dot32(upper, v_done())


def on_device(
    n,
    m,
    genotype,
    freqs,
    left_factors,
    singular,
    right_factors,
    sketch,
    batch_sizes,
    missing_batch,
    missing_block,
):
    rows, cols = genotype.shape
    k = sketch.shape[1]
    rank = left_factors.shape[1]
    depth = -(-rank // 32) * 32
    width = cols // n
    held = -(-rank // 8) * 8
    f32, b16 = jnp.float32, jnp.bfloat16
    vm = pl.BlockSpec(memory_space=pltpu.VMEM)
    dma = pltpu.SemaphoreType.DMA
    loops = ITERS + 1
    basis_t, proj_t, snpb_t = pl.pallas_call(
        functools.partial(
            kernel,
            n,
            m,
            float(rows * n),
            float(cols * m),
        ),
        out_shape=(
            pltpu.VMEM((k, rows), f32),
            pltpu.VMEM((k, cols), f32),
            pltpu.VMEM((k, cols), f32),
        ),
        in_specs=[pl.BlockSpec(memory_space=pl.ANY)] * 9,
        out_specs=(vm, vm, vm),
        scratch_shapes=[
            pltpu.VMEM((rows, cols), jnp.int32),
            pltpu.SMEM(singular.shape, f32),
            pltpu.SMEM(batch_sizes.shape, jnp.int32),
            pltpu.SMEM(missing_batch.shape, jnp.int32),
            pltpu.SMEM(missing_block.shape, jnp.int32),
            pltpu.VMEM((1, cols), f32),
            pltpu.VMEM((rank, rows), f32),
            pltpu.VMEM((rank, width), f32),
            pltpu.VMEM((k, cols), b16),
            pltpu.VMEM((depth, rows), f32),
            pltpu.VMEM((held, width), f32),
            pltpu.VMEM((cols, k), b16),
            pltpu.VMEM((rows, 6 * depth), b16),
            pltpu.VMEM((rows, 128), f32),
            pltpu.VMEM((rows, cols), b16),
            pltpu.VMEM((2, n // 2, held, width), f32),
            pltpu.VMEM((6 * depth, cols), b16),
            pltpu.VMEM((m, k, rows), b16),
            pltpu.VMEM((ITERS, m, k, rows), f32),
            pltpu.VMEM((ITERS, m, k, k), f32),
            pltpu.VMEM((loops, n // 2, k, width), f32),
            pltpu.VMEM((loops, n // 2, k, width), f32),
            pltpu.VMEM((ITERS, n // 2, k, width), f32),
            pltpu.VMEM((ITERS, n // 2, k, width), f32),
            pltpu.VMEM((n // 2, k, width), b16),
            pltpu.VMEM((n // 2, k, width), b16),
            pltpu.VMEM((loops, k // 2, 2 * k), f32),
            pltpu.VMEM((loops, k // 2, 2 * k), f32),
            pltpu.VMEM((loops, n // 2, k // 2, 2 * k), f32),
            pltpu.VMEM((loops, 2, n // 2, k, width), b16),
            pltpu.VMEM((2, k, cols // 2), b16),
            dma((rows // ROW_STEP,)),
            dma((8,)),
            dma((n // 2,)),
            dma((n // 2,)),
            dma,
            dma,
            dma((loops, m)),
            dma((loops, m)),
            dma((ITERS, m)),
            dma((ITERS, m)),
            dma((loops,)),
            dma((loops,)),
            dma((loops, n // 2)),
            dma((loops, n // 2)),
            dma((loops,)),
            dma((loops,)),
            dma((loops,)),
            dma((loops,)),
            dma((loops, n // 2)),
            dma((loops, n // 2)),
            dma((loops, n // 2)),
            dma((loops, n // 2)),
        ],
        compiler_params=pltpu.CompilerParams(
            collective_id=0, has_side_effects=True, vmem_limit_bytes=60 * 1024 * 1024
        ),
        cost_estimate=pl.CostEstimate(
            flops=12 * rows * cols * k, bytes_accessed=4 * rows * cols, transcendentals=0
        ),
    )(
        genotype,
        freqs[None, :],
        left_factors.T,
        right_factors.T,
        sketch.T,
        singular,
        batch_sizes,
        missing_batch,
        missing_block,
    )
    return basis_t.T, proj_t.T, snpb_t.T


def solution(mesh):
    in_specs = (
        P("samp", "snp"),
        P("snp"),
        P("samp", None),
        P(),
        P(("snp", "samp"), None),
        P("snp", None),
        P(),
        P(),
        P(),
    )
    out_specs = (P("samp", None), P("snp", None), P("snp", None))
    body = functools.partial(on_device, mesh.shape["samp"], mesh.shape["snp"])
    return jax.shard_map(
        body, mesh=mesh, in_specs=in_specs, out_specs=out_specs, check_vma=False
    )
```
